256 devices in a mesh: grp: 4 (over y_hi, core), blk: 64 (over x, y_lo, z).
Axes of the slice: x: 4, y: 4 (y_hi: 2, y_lo: 2; y = y_hi * 2 + y_lo), z: 8, core: 2. Of those that a mesh axis runs over, the one named last changes fastest.
Arguments:
- main_hidden: bfloat16 [8192, 3072], P('blk', 'grp'), may hold values from -6 to 6
- ctrl_query: bfloat16 [8192, 1536], P('blk', 'grp'), may hold values from -150 to 150
- ctrl_key: bfloat16 [8192, 1536], P('blk', 'grp'), may hold values from -6 to 6
- ctrl_value: bfloat16 [8192, 1536], P('blk', 'grp'), may hold values from -6 to 6
- w_out: bfloat16 [1536, 3072], P('grp'), may hold values from -1 to 1
- d_mixed: bfloat16 [8192, 3072], P('blk', 'grp'), may hold values from -3 to 3
- control_slot: int32 [8192], P('blk'), may hold values from 0 to 8191, as said below
Outputs:
- main_mixed: bfloat16 [8192, 3072], P('blk', 'grp')
- d_query: bfloat16 [8192, 1536], P('blk', 'grp')
- d_key: bfloat16 [8192, 1536], P('blk', 'grp')
- d_value: bfloat16 [8192, 1536], P('blk', 'grp')
- d_w_out: float32 [1536, 3072], P('grp', 'blk')
The draws below stay inside these ranges and needn't reach their ends.
Inputs may be any that keep to these rules, and one draw needn't show every extreme that they name: `control_slot`: A permutation of the token positions. Every aligned block of 128 entries sends exactly 2 of its tokens into each aligned block of 128 control positions.
All inputs are finite; a program needn't handle non-finite values.
Results may differ from the reference program's by a relative error of at most 0.038.
Values may be sent and summed in bfloat16 or wider, within the bound.
No kernel may reach another device: no remote copies, remote signals or barrier semaphores. Data moves between devices by JAX's collectives and lax.ppermute only.
A program may use at most 128 MiB of HBM per device.

```python
import math
import jax
import jax.numpy as jnp
from jax import lax

D = 3072
HD = 128
HEAD_GRP = 3
TOK_DEV = 128
HEADS = 12
HC = 1536
SEQ = 8192
N_GRP = 4


def shared_keys(key):
    return jnp.clip(jax.random.normal(key, (SEQ, HEADS * HD), jnp.float32), -6.0, 6.0)


def draw_ctrl_key(key, part):
    shared = shared_keys(key)
    return shared.astype(jnp.bfloat16)


def draw_ctrl_query(key, part):
    key = jax.random.fold_in(key, 23)
    drawn_rows = 2.0 * jnp.clip(jax.random.normal(key, (SEQ, HEADS * HD), jnp.float32), -6.0, 6.0)
    return drawn_rows.astype(jnp.bfloat16)


def draw_control_slot(key, part):
    key = jax.random.fold_in(key, 37)
    key_peers, key_slots = jax.random.split(key)
    blocks = SEQ // TOK_DEV
    per_peer = TOK_DEV // blocks
    peer_scores = jax.random.randint(key_peers, (blocks, blocks), 0, 1 << 16) * blocks + jnp.arange(blocks)[None, :]
    peer_order = jnp.argsort(peer_scores, axis=1).astype(jnp.int32)
    slot_scores = jax.random.randint(key_slots, (blocks, TOK_DEV), 0, 1 << 12) * TOK_DEV + jnp.arange(TOK_DEV)[None, :]
    slot_order = jnp.argsort(slot_scores, axis=1).astype(jnp.int32)
    positions = jnp.arange(SEQ)
    source = positions // TOK_DEV
    local = positions % TOK_DEV
    target = peer_order[source, local // per_peer]
    within = slot_order[target, source * per_peer + local % per_peer]
    return (target * TOK_DEV + within).astype(jnp.int32)


def shard_levels(own_key, shape, shards, low, high):
    def one(dim, blocks):
        steps = jax.random.uniform(jax.random.fold_in(jax.random.fold_in(own_key, 6), dim), (blocks,), jnp.float32, low / len(shards), high / len(shards))
        return jnp.repeat(jnp.exp(steps), shape[dim] // blocks).reshape((-1,) + (1,) * (len(shape) - dim - 1))

    level = one(*shards[0])
    for cut in shards[1:]:
        level = level * one(*cut)
    return level


def bell_draw(own_key, extent, scale, reach, shards=(), dtype=jnp.bfloat16):
    loudness = shard_levels(own_key, extent, shards, -0.22, 0.18) if shards else 1.0
    result = jax.random.normal(own_key, extent, jnp.float32) * scale * loudness
    return jnp.minimum(jnp.maximum(result, -reach), reach).astype(dtype)


def setup_inputs(seed: int = 0) -> dict:
    splits = jax.random.split(jax.random.key(seed), 8)
    return {
        "main_hidden": bell_draw(splits[0], (SEQ, D), 0.5, 6.0, ((0, 64), (1, 4))),
        "ctrl_query": draw_ctrl_query(jax.random.fold_in(splits[7], 71), 0),
        "ctrl_key": draw_ctrl_key(jax.random.fold_in(splits[7], 71), 0),
        "ctrl_value": bell_draw(splits[3], (SEQ, HC), 1.0, 6.0, ((0, 64), (1, 4))),
        "w_out": bell_draw(splits[4], (HC, D), (3.0 * HC ** -0.5), 1.0, ((0, 4),)),
        "d_mixed": bell_draw(splits[5], (SEQ, D), 0.2, 3.0, ((0, 64), (1, 4))),
        "control_slot": draw_control_slot(jax.random.fold_in(splits[7], 71), 0),
    }


def split_heads(matrix):
    return matrix.reshape(SEQ, HEADS, HD).transpose(1, 0, 2)

def merge_heads(tensor):
    return tensor.transpose(1, 0, 2).reshape(SEQ, HEADS * HD)

def reference(main_hidden, ctrl_query, ctrl_key, ctrl_value, w_out, d_mixed, control_slot):
    score_scale = 1.0 / math.sqrt(HD)
    block_rows = min(512, SEQ)
    block_count = SEQ // block_rows
    query_heads = split_heads(ctrl_query)
    key_heads = split_heads(ctrl_key)
    value_heads = split_heads(ctrl_value)

    def head_forward(operands):
        query_one, key_one, value_one = operands

        def one_block(query_rows):
            scores = jnp.dot(query_rows, key_one.T, preferred_element_type=jnp.float32) * score_scale
            row_peak = lax.optimization_barrier(jnp.max(scores, axis=1, keepdims=True))
            log_norm = row_peak + jnp.log(lax.optimization_barrier(jnp.sum(jnp.exp(scores - row_peak), axis=1, keepdims=True)))
            soft_weights = jnp.exp(scores - log_norm).astype(jnp.bfloat16)
            return (jnp.dot(soft_weights, value_one, preferred_element_type=jnp.float32), log_norm[:, 0])
        outputs, log_norm = lax.map(one_block, query_one.reshape(block_count, block_rows, HD))
        return (outputs.reshape(SEQ, HD), log_norm.reshape(SEQ))
    head_out, log_norms = lax.map(head_forward, (query_heads, key_heads, value_heads))
    attended = merge_heads(head_out).astype(jnp.bfloat16)
    head_cols = HEAD_GRP * HD
    residual = jnp.zeros((SEQ, D), jnp.float32)
    for group_idx in range(N_GRP):
        lower = group_idx * head_cols
        partial_term = jnp.dot(attended[:, lower:lower + head_cols], w_out[lower:lower + head_cols], preferred_element_type=jnp.float32).astype(jnp.bfloat16)
        residual = residual + lax.optimization_barrier(partial_term).astype(jnp.float32)
    main_mixed = (main_hidden.astype(jnp.float32) + residual[control_slot]).astype(jnp.bfloat16)
    d_control = jnp.zeros((SEQ, D), jnp.bfloat16).at[control_slot].set(d_mixed)
    d_attended = jnp.dot(d_control, w_out.T, preferred_element_type=jnp.float32).astype(jnp.bfloat16)
    d_w_out = jnp.dot(attended.T, d_control, preferred_element_type=jnp.float32)
    row_delta = lax.optimization_barrier(jnp.sum((d_attended.astype(jnp.float32) * attended.astype(jnp.float32)).reshape(SEQ, HEADS, HD), axis=2)).T
    d_heads = split_heads(d_attended)

    def head_backward(operands):
        query_one, key_one, value_one, grad_one, norm_one, delta_one = operands

        def one_block(totals, block_data):
            key_grad, value_grad = totals
            query_rows, grad_rows, norm_rows, delta_rows = block_data
            scores = jnp.dot(query_rows, key_one.T, preferred_element_type=jnp.float32) * score_scale
            soft_weights = jnp.exp(scores - norm_rows[:, None])
            d_probs = jnp.dot(grad_rows, value_one.T, preferred_element_type=jnp.float32)
            d_scores = (soft_weights * (d_probs - delta_rows[:, None])).astype(jnp.bfloat16)
            query_grad = jnp.dot(d_scores, key_one, preferred_element_type=jnp.float32) * score_scale
            key_grad = key_grad + jnp.dot(d_scores.T, query_rows, preferred_element_type=jnp.float32) * score_scale
            value_grad = value_grad + jnp.dot(soft_weights.astype(jnp.bfloat16).T, grad_rows, preferred_element_type=jnp.float32)
            return ((key_grad, value_grad), query_grad)
        zero_rows = jnp.zeros((SEQ, HD), jnp.float32)
        blocks_in = (query_one.reshape(block_count, block_rows, HD), grad_one.reshape(block_count, block_rows, HD), norm_one.reshape(block_count, block_rows), delta_one.reshape(block_count, block_rows))
        (key_grad, value_grad), query_grad = lax.scan(one_block, (zero_rows, zero_rows), blocks_in)
        return (query_grad.reshape(SEQ, HD), key_grad, value_grad)
    query_grad, key_grad, value_grad = lax.map(head_backward, (query_heads, key_heads, value_heads, d_heads, log_norms, row_delta))
    return (main_mixed, merge_heads(query_grad).astype(jnp.bfloat16), merge_heads(key_grad).astype(jnp.bfloat16), merge_heads(value_grad).astype(jnp.bfloat16), d_w_out)
```

```python
import math

import jax
import jax.numpy as jnp
from jax import lax
from jax.experimental import pallas as pl
from jax.experimental.pallas import tpu as pltpu
from jax.sharding import Mesh
from jax.sharding import PartitionSpec as P

HD = 128
HEADS = 3
COLS = HEADS * HD
TOK = 128
SIDE = 8
TILE = TOK * SIDE
QB = 256
SCALE = 1.0 / math.sqrt(HD)
LOG2E = math.log2(math.e)
PEER = TOK // SIDE
SPAN = 768
QUAD = ("x", "yl")
F32 = jnp.float32
BF16 = jnp.bfloat16
NT = (((1,), (1,)), ((), ()))
TN = (((0,), (0,)), ((), ()))
VMEM = pl.BlockSpec(memory_space=pltpu.VMEM)
SMEM = pl.BlockSpec(memory_space=pltpu.SMEM)
PARAMS = pltpu.CompilerParams(vmem_limit_bytes=48 * 1024 * 1024)
RING = (0, -1, 1, -2, 2, -3, 3, 4)


def dot(left, right, dims=(((1,), (0,)), ((), ()))):
    return lax.dot_general(left, right, dims, preferred_element_type=F32)


def call(body, out, *args, specs=None):
    return pl.pallas_call(
        body,
        out_shape=[jax.ShapeDtypeStruct(shape, dtype) for shape, dtype in out],
        in_specs=specs or [VMEM] * len(args),
        out_specs=[VMEM] * len(out),
        compiler_params=PARAMS,
    )(*args)


def head(idx):
    return slice(idx * HD, (idx + 1) * HD)


def block_of(slot):
    return (slot >> 7) & (SIDE - 1)


def project_body(d_ref, w_ref, row_ref, col_ref, pay_ref, cut_ref):
    total = jnp.zeros((TOK, COLS), F32)
    for part in range(4):
        total += dot(d_ref[part], w_ref[:, part * SPAN : (part + 1) * SPAN], NT)
        for half in range(2):
            cut_ref[2 * part + half] = d_ref[part][:, half * COLS : (half + 1) * COLS]
    slot_row, slot_col = row_ref[...], col_ref[...]
    first = lax.broadcasted_iota(jnp.int32, (TOK, TOK), 0)
    second = lax.broadcasted_iota(jnp.int32, (TOK, TOK), 1)
    same = (block_of(slot_row) == block_of(slot_col)) & (first < second)
    ahead = jnp.sum(jnp.where(same, 1.0, 0.0), axis=0, keepdims=True).astype(jnp.int32)
    rank = block_of(slot_row) * PEER + ahead
    order = jnp.where(first == rank, 1.0, 0.0).astype(BF16)
    place = jnp.where(
        second == 0,
        (slot_col >> 10).astype(F32),
        jnp.where(second == 1, (slot_col & (TOK - 1)).astype(F32), 0.0),
    )
    pay_ref[:, :COLS] = dot(order, total.astype(BF16)).astype(BF16)
    pay_ref[:, COLS:] = dot(order, place.astype(BF16)).astype(BF16)


def forward_body(q_ref, kv_ref, out_ref, lse_ref):
    lse_ref[...] = jnp.zeros_like(lse_ref)
    for idx in range(HEADS):
        keys = kv_ref[:, head(idx)]
        values_t = kv_ref[:, head(HEADS + idx)].T
        for start in range(0, TILE, QB):
            cols = slice(start, start + QB)
            scores = dot(keys, q_ref[cols, head(idx)], NT)
            peak = jnp.max(scores, axis=0, keepdims=True)
            weights = jnp.exp2((scores - peak) * (SCALE * LOG2E))
            total = jnp.sum(weights, axis=0, keepdims=True)
            out_ref[head(idx), cols] = dot(values_t, weights.astype(BF16)) / total
            lse_ref[idx : idx + 1, cols] = peak * SCALE + jnp.log(total)


def places(arrived_ref):
    place = arrived_ref[:, COLS : COLS + HD].astype(F32)
    target = place[:, 0:1] * float(TOK) + place[:, 1:2]
    lanes = lax.broadcasted_iota(jnp.int32, (TILE, TILE), 1)
    return jnp.where(lanes == target.astype(jnp.int32), 1.0, 0.0).astype(BF16)


def delta_body(arrived_ref, out_ref, lse_ref, grad_ref, stat_ref):
    order = places(arrived_ref)
    stat_ref[...] = lse_ref[...]
    for idx in range(HEADS):
        grad_t = dot(arrived_ref[:, head(idx)].T, order)
        grad_ref[:, head(idx)] = grad_t.T.astype(BF16)
        stat_ref[HEADS + idx : HEADS + idx + 1, :] = jnp.sum(
            grad_t * out_ref[head(idx), :], axis=0, keepdims=True
        )


def merge_body(all_ref, stat_ref, out_ref, arrived_ref, norm_ref, part_ref):
    order = places(arrived_ref)
    norm_ref[...] = jnp.zeros_like(norm_ref)
    for idx in range(HEADS):
        lses = [all_ref[SIDE * s + idx : SIDE * s + idx + 1, :] for s in range(SIDE)]
        peak = lses[0]
        for one in lses[1:]:
            peak = jnp.maximum(peak, one)
        total = jnp.zeros_like(peak)
        delta = jnp.zeros_like(peak)
        for s, one in enumerate(lses):
            weight = jnp.exp(one - peak)
            total += weight
            row = SIDE * s + HEADS + idx
            delta += weight * all_ref[row : row + 1, :]
        norm = peak + jnp.log(total)
        norm_ref[idx : idx + 1, :] = norm
        norm_ref[HEADS + idx : HEADS + idx + 1, :] = delta / total
        share = jnp.exp(stat_ref[idx : idx + 1, :] - norm)
        scaled = (out_ref[head(idx), :] * share).astype(BF16)
        part_ref[:, head(idx)] = dot(scaled, order, NT).T.astype(BF16)


def backward_body(z_ref, q_ref, kv_ref, grad_ref, norm_ref, dq_ref, dkv_ref):
    z_pos = z_ref[0]
    for idx in range(HEADS):
        keys = kv_ref[:, head(idx)]
        keys_t = keys.T
        values = kv_ref[:, head(HEADS + idx)]
        d_keys = jnp.zeros((TILE, HD), F32)
        d_values = jnp.zeros((TILE, HD), F32)
        for start in range(0, TILE, QB):
            cols = slice(start, start + QB)
            query = q_ref[cols, head(idx)]
            grad = grad_ref[cols, head(idx)]
            scores = dot(keys, query, NT) * SCALE
            weights = jnp.exp2((scores - norm_ref[idx : idx + 1, cols]) * LOG2E)
            d_probs = dot(values, grad, NT)
            d_scores = (weights * (d_probs - norm_ref[HEADS + idx : HEADS + idx + 1, cols])).astype(BF16)
            d_values += dot(weights.astype(BF16), grad)
            d_keys += dot(d_scores, query)
            dq_ref[cols, head(idx)] = (dot(keys_t, d_scores) * SCALE).T.astype(BF16)
        d_keys = (d_keys * SCALE).astype(BF16)
        d_values = d_values.astype(BF16)
        for spot, offset in enumerate(RING):
            rows = slice(spot * TOK, (spot + 1) * TOK)
            owner = lax.rem(z_pos + (offset + SIDE), SIDE)
            here = pl.ds(pl.multiple_of(owner * TOK, TOK), TOK)
            dkv_ref[here, head(idx)] = d_keys[rows]
            dkv_ref[here, head(HEADS + idx)] = d_values[rows]


def output_body(sorted_ref, w_ref, row_ref, col_ref, att_ref, part_ref):
    slot_row, slot_col = row_ref[...], col_ref[...]
    first = lax.broadcasted_iota(jnp.int32, (TOK, TOK), 0)
    second = lax.broadcasted_iota(jnp.int32, (TOK, TOK), 1)
    same = (block_of(slot_row) == block_of(slot_col)) & (second < first)
    ahead = jnp.sum(jnp.where(same, 1.0, 0.0), axis=1, keepdims=True).astype(jnp.int32)
    rank = block_of(slot_col) * PEER + ahead
    order = jnp.where(second == rank, 1.0, 0.0).astype(BF16)
    attended = dot(order, sorted_ref[...]).astype(BF16)
    att_ref[...] = attended
    for part in range(4):
        part_ref[part] = dot(attended, w_ref[:, part * SPAN : (part + 1) * SPAN]).astype(BF16)


def shift(value, axis, step, size):
    return lax.ppermute(value, axis, [(i, (i + step) % size) for i in range(size)])


def exchange(value, axis):
    return lax.all_to_all(value, axis, split_axis=0, concat_axis=0, tiled=True)


def gather_quad(value):
    return exchange(jnp.tile(value, (SIDE, 1)), QUAD)


def ring_gather(value):
    ahead = back = value
    blocks = [value]
    for _ in range(3):
        ahead, back = shift(ahead, "z", 1, SIDE), shift(back, "z", SIDE - 1, SIDE)
        blocks += [ahead, back]
    half = TOK // 2
    blocks += [shift(ahead[:half], "z", 1, SIDE), shift(back[half:], "z", SIDE - 1, SIDE)]
    return jnp.concatenate(blocks, axis=0)


def pick(value, idx, axis):
    return lax.dynamic_index_in_dim(value, idx, axis, keepdims=False)


def on_device(main_hidden, ctrl_query, ctrl_key, ctrl_value, w_out, d_mixed, control_slot):
    y_pos, core, z_pos = lax.axis_index("yh"), lax.axis_index("co"), lax.axis_index("z")
    slot_row, slot_col = control_slot.reshape(1, TOK), control_slot.reshape(TOK, 1)

    other = shift(d_mixed, "yh", 1, 2)
    pair = jnp.where(y_pos == 0, jnp.stack([d_mixed, other]), jnp.stack([other, d_mixed]))
    other = shift(pair, "co", 1, 2)
    d_full = jnp.where(core == 0, jnp.stack([pair, other], 1), jnp.stack([other, pair], 1))
    d_full = d_full.reshape(4, TOK, SPAN)

    key_value = ring_gather(jnp.concatenate([ctrl_key, ctrl_value], axis=1))
    query = gather_quad(ctrl_query)

    payload, d_cut = call(
        project_body,
        [((TOK, COLS + HD), BF16), ((SIDE, TOK, COLS), BF16)],
        d_full,
        w_out,
        slot_row,
        slot_col,
    )
    arrived = gather_quad(exchange(payload, "z"))

    out_t, lse = call(forward_body, [((COLS, TILE), F32), ((SIDE, TILE), F32)], query, key_value)
    grad, stats = call(
        delta_body, [((TILE, COLS), BF16), ((SIDE, TILE), F32)], arrived, out_t, lse
    )
    all_stats = gather_quad(stats)
    norms, part = call(
        merge_body, [((SIDE, TILE), F32), ((TILE, COLS), BF16)], all_stats, stats, out_t, arrived
    )
    d_query, d_key_value = call(
        backward_body,
        [((TILE, COLS), BF16), ((TILE, 2 * COLS), BF16)],
        z_pos.reshape(1).astype(jnp.int32),
        query,
        key_value,
        grad,
        norms,
        specs=[SMEM, VMEM, VMEM, VMEM, VMEM],
    )
    d_key_value = lax.psum_scatter(d_key_value, "z", scatter_dimension=0, tiled=True)

    attended = jnp.sum(exchange(part, QUAD).reshape(SIDE, TOK, COLS).astype(F32), axis=0)
    attended = exchange(attended.astype(BF16), "z")
    attended, partial_out = call(
        output_body,
        [((TOK, COLS), BF16), ((4, TOK, SPAN), BF16)],
        attended,
        w_out,
        slot_row,
        slot_col,
    )

    by_core = partial_out.reshape(2, 2, TOK, SPAN)
    summed = pick(by_core, core, 1).astype(F32) + shift(
        pick(by_core, 1 - core, 1), "co", 1, 2
    ).astype(F32)
    residual = pick(summed, y_pos, 0) + shift(
        pick(summed, 1 - y_pos, 0).astype(BF16), "yh", 1, 2
    ).astype(F32)
    main_mixed = (main_hidden.astype(F32) + residual).astype(BF16)

    d_query = jnp.sum(exchange(d_query, QUAD).reshape(SIDE, TOK, COLS).astype(F32), axis=0)

    d_cut = exchange(d_cut, QUAD).reshape(TILE, COLS)
    d_w_out = dot(d_cut, gather_quad(attended), TN).astype(BF16)
    d_w_out = exchange(d_w_out, "z").reshape(SIDE, COLS // SIDE, COLS)
    d_w_out = jnp.sum(d_w_out.astype(F32), axis=0).T
    return (
        main_mixed,
        d_query.astype(BF16),
        d_key_value[:, :COLS],
        d_key_value[:, COLS:],
        d_w_out,
    )


def solution(mesh):
    fine = Mesh(mesh.devices.reshape(2, 2, 4, 2, 8), ("yh", "co", "x", "yl", "z"))
    grp, blk = ("yh", "co"), ("x", "yl", "z")
    in_specs = (
        P(blk, grp),
        P(blk, grp),
        P(blk, grp),
        P(blk, grp),
        P(grp, None),
        P(blk, grp),
        P(blk),
    )
    out_specs = (
        P(blk, grp),
        P(blk, grp),
        P(blk, grp),
        P(blk, grp),
        P(grp, blk),
    )
    return jax.shard_map(
        on_device, mesh=fine, in_specs=in_specs, out_specs=out_specs, check_vma=False
    )
```

```python
import math

import jax
import jax.numpy as jnp
from jax import lax
from jax.experimental import pallas as pl
from jax.experimental.pallas import tpu as pltpu
from jax.sharding import Mesh
from jax.sharding import PartitionSpec as P

HD = 128
HEADS = 3
COLS = HEADS * HD
TOK = 128
SIDE = 8
TILE = TOK * SIDE
QB = 256
SCALE = 1.0 / math.sqrt(HD)
LOG2E = math.log2(math.e)
PEER = TOK // SIDE
SPAN = 768
QUAD = ("x", "yl")
F32 = jnp.float32
BF16 = jnp.bfloat16
NT = (((1,), (1,)), ((), ()))
TN = (((0,), (0,)), ((), ()))
HBM = pl.BlockSpec(memory_space=pltpu.HBM)
VMEM = pl.BlockSpec(memory_space=pltpu.VMEM)
SMEM = pl.BlockSpec(memory_space=pltpu.SMEM)
MIB = 1024 * 1024
STAT = 16
SLAB = TOK + 3 * STAT


def dot(left, right, dims=(((1,), (0,)), ((), ()))):
    return lax.dot_general(left, right, dims, preferred_element_type=F32)


def far(array, parts=1):
    return array, parts


def block_copies(source, dest, sems, first, parts):
    width = source.shape[-1] // parts
    found = []
    for n in range(parts):
        here, there = source, dest
        if parts > 1:
            here, there = (r.at[:, n * width : (n + 1) * width] for r in (source, dest))
        found.append(pltpu.make_async_copy(here, there, sems.at[first + n]))
    return found


def call(body, out, *args, mib, stack=None):
    arg_parts = [arg[1] if isinstance(arg, tuple) else 0 for arg in args]
    args = [arg[0] if isinstance(arg, tuple) else arg for arg in args]
    out_parts = [one[1] if isinstance(one[1], int) else 0 for one in out]
    out = [one[0] if isinstance(one[1], int) else one for one in out]
    n_in, n_out = len(args), len(out)
    far_in = [i for i in range(n_in) if arg_parts[i]]
    far_out = [i for i in range(n_out) if out_parts[i]]
    n_load, n_store = sum(arg_parts), sum(out_parts)

    def kernel(*refs):
        ins, outs = list(refs[:n_in]), list(refs[n_in : n_in + n_out])
        rest = list(refs[n_in + n_out :])
        if stack:
            pieces, rest = rest[:SIDE], rest[SIDE:]
            piece_sem, whole = rest.pop(), rest.pop()
            outs.append(whole)
        loads, stores = {}, {}
        load_sem = rest.pop(0) if n_load else None
        store_sem = rest.pop(0) if n_store else None
        first = 0
        for i in far_in:
            spot = rest.pop(0)
            loads[i] = block_copies(ins[i], spot, load_sem, first, arg_parts[i])
            first += arg_parts[i]
            ins[i] = spot
        first = 0
        for i in far_out:
            spot = rest.pop(0)
            stores[i] = block_copies(spot, outs[i], store_sem, first, out_parts[i])
            first += out_parts[i]
            outs[i] = spot
        for n in range(max(arg_parts)):
            for i in far_in:
                if n < arg_parts[i]:
                    loads[i][n].start()
        for i in far_in:
            if arg_parts[i] == 1:
                loads[i][0].wait()
        started = set()

        def ready(i, n):
            loads[i][n].wait()

        def done(i, n):
            stores[i][n].start()
            started.add((i, n))

        steps = (ready, done) if max(arg_parts) > 1 or max(out_parts) > 1 else ()
        body(*steps, *ins, *outs, *rest)
        for i in far_out:
            for n in range(out_parts[i]):
                if (i, n) not in started:
                    stores[i][n].start()
        if stack:
            stores[n_out] = [
                pltpu.make_async_copy(
                    whole.at[rows_of(around(ins[0][0], step)), :], piece, piece_sem.at[step]
                )
                for step, piece in enumerate(pieces)
            ]
            for copy in stores[n_out]:
                copy.start()
        for i in stores:
            for copy in stores[i]:
                copy.wait()

    dma = pltpu.SemaphoreType.DMA
    return pl.pallas_call(
        kernel,
        out_shape=[
            pltpu.HBM(*one) if out_parts[i] else jax.ShapeDtypeStruct(*one)
            for i, one in enumerate(out)
        ]
        + ([pltpu.HBM((TOK, stack), BF16)] * SIDE if stack else []),
        in_specs=[
            HBM if arg_parts[i] else SMEM if args[i].shape == (1,) else VMEM for i in range(n_in)
        ],
        out_specs=[HBM if parts else VMEM for parts in out_parts] + ([HBM] * SIDE if stack else []),
        scratch_shapes=[
            *([dma((n_load,))] if n_load else []),
            *([dma((n_store,))] if n_store else []),
            *[pltpu.VMEM(args[i].shape, args[i].dtype) for i in far_in],
            *[pltpu.VMEM(*out[i]) for i in far_out],
            *([pltpu.VMEM((TILE, stack), BF16), dma((SIDE,))] if stack else []),
        ],
        compiler_params=pltpu.CompilerParams(vmem_limit_bytes=mib * MIB),
    )(
        *[
            pltpu.with_memory_space_constraint(arg, pltpu.HBM) if arg_parts[i] else arg
            for i, arg in enumerate(args)
        ]
    )


def around(pos, step):
    return lax.rem(pos + (step + SIDE), SIDE)


def rows_of(pos):
    return pl.ds(pl.multiple_of(pos * TOK, TOK), TOK)


def head(idx):
    return slice(idx * HD, (idx + 1) * HD)


def block_of(slot):
    return (slot >> 7) & (SIDE - 1)


def sorted_by_block(slot_row):
    first = lax.broadcasted_iota(jnp.int32, (TOK, TOK), 0)
    second = lax.broadcasted_iota(jnp.int32, (TOK, TOK), 1)
    spread = jnp.where(first == second, slot_row.astype(F32), 0.0)
    slot_col = jnp.sum(spread, axis=1, keepdims=True).astype(jnp.int32)
    same = (block_of(slot_row) == block_of(slot_col)) & (first < second)
    ahead = jnp.sum(jnp.where(same, 1.0, 0.0), axis=0, keepdims=True).astype(jnp.int32)
    rank = block_of(slot_row) * PEER + ahead
    order = jnp.where(first == rank, 1.0, 0.0).astype(BF16)
    place = jnp.where(
        second == 0,
        (slot_col >> 10).astype(F32),
        jnp.where(second == 1, (slot_col & (TOK - 1)).astype(F32), 0.0),
    )
    return order, place


def project_body(
    y_ref, core_ref, d0_ref, d1_ref, d2_ref, d3_ref, w_ref, row_ref, pay_ref, cut_ref
):
    y_pos, core = y_ref[0], core_ref[0]
    order, place = sorted_by_block(row_ref[...])
    total = jnp.zeros((TOK, COLS), F32)
    pieces = (
        (d0_ref, y_pos, core),
        (d1_ref, 1 - y_pos, core),
        (d2_ref, y_pos, 1 - core),
        (d3_ref, 1 - y_pos, 1 - core),
    )
    for d_ref, along, across in pieces:
        part = 2 * along + across
        here = pl.ds(pl.multiple_of(part * SPAN, SPAN), SPAN)
        total += dot(d_ref[...], w_ref[:, here], NT)
        rows = dot(order, d_ref[...]).astype(BF16)
        cut_ref[2 * part] = rows[:, :COLS]
        cut_ref[2 * part + 1] = rows[:, COLS:]
    pay_ref[:, :COLS] = dot(order, total.astype(BF16)).astype(BF16)
    pay_ref[:, COLS:] = dot(order, place.astype(BF16)).astype(BF16)


def forward_body(ready, done, q_ref, kv_ref, out_ref, lse_ref):
    lse_ref[...] = jnp.zeros_like(lse_ref)
    for idx in range(HEADS):
        ready(0, idx)
        ready(1, idx)
        ready(1, HEADS + idx)
        keys = kv_ref[:, head(idx)]
        values_t = kv_ref[:, head(HEADS + idx)].T
        for start in range(0, TILE, QB):
            cols = slice(start, start + QB)
            scores = dot(keys, q_ref[cols, head(idx)], NT)
            peak = jnp.max(scores, axis=0, keepdims=True)
            weights = jnp.exp2((scores - peak) * (SCALE * LOG2E))
            total = jnp.sum(weights, axis=0, keepdims=True)
            out_ref[head(idx), cols] = (dot(values_t, weights.astype(BF16)) / total).astype(BF16)
            lse_ref[idx : idx + 1, cols] = peak * SCALE + jnp.log(total)


def places(arrived):
    place = arrived.astype(F32)
    target = place[:, 0:1] * float(TOK) + place[:, 1:2]
    lanes = lax.broadcasted_iota(jnp.int32, (place.shape[0], TILE), 1)
    return jnp.where(lanes == target.astype(jnp.int32), 1.0, 0.0).astype(BF16)


def terms(value, count):
    found = []
    for _ in range(count):
        found.append(value.astype(BF16))
        value = value - found[-1].astype(F32)
    return found


def delta_body(ready, done, arrived_ref, out_ref, lse_ref, grad_ref, send_ref):
    order = places(arrived_ref[:, COLS:])
    deltas = []
    for idx in range(HEADS):
        grad_t = dot(arrived_ref[:, head(idx)].T, order)
        grad_ref[:, head(idx)] = grad_t.T.astype(BF16)
        done(0, idx)
        deltas.append(jnp.sum(grad_t * out_ref[head(idx), :].astype(F32), axis=0, keepdims=True))
        rows = dot(out_ref[head(idx), :], order, NT).T.astype(BF16)
        for peer in range(SIDE):
            send_ref[peer, :TOK, head(idx)] = rows[peer * TOK : (peer + 1) * TOK]
    zero = jnp.zeros((1, TILE), BF16)
    stats = [t for t in terms(lse_ref[:HEADS, :], 3)]
    stats += terms(jnp.concatenate(deltas, axis=0), 2)
    stats = jnp.concatenate([t.astype(F32) for t in stats] + [zero.astype(F32)], axis=0).astype(BF16)
    for peer in range(SIDE):
        for n, start in enumerate(range(0, TILE, COLS)):
            width = min(COLS, TILE - start)
            send_ref[peer, TOK + STAT * n : TOK + STAT * (n + 1), :width] = stats[:, start : start + width]


def merge_body(quad_ref, all_ref, arrived_ref, norm_ref, att_ref):
    lses, deltas = [], []
    for peer in range(SIDE):
        parts = []
        for n, start in enumerate(range(0, TILE, COLS)):
            width = min(COLS, TILE - start)
            parts.append(all_ref[peer, TOK + STAT * n : TOK + STAT * (n + 1), :width].astype(F32))
        stats = jnp.concatenate(parts, axis=1)
        lses.append(stats[0:3] + stats[3:6] + stats[6:9])
        deltas.append(stats[9:12] + stats[12:15])
    peak = lses[0]
    for one in lses[1:]:
        peak = jnp.maximum(peak, one)
    weights = [jnp.exp(one - peak) for one in lses]
    total = sum(weights)
    norm_ref[...] = jnp.zeros_like(norm_ref)
    norm_ref[:HEADS, :] = peak + jnp.log(total)
    norm_ref[HEADS : 2 * HEADS, :] = sum(w * d for w, d in zip(weights, deltas)) / total
    shares = jnp.concatenate([w / total for w in weights], axis=0)
    mine = places(arrived_ref[rows_of(quad_ref[0]), COLS:])
    shares = sum(dot(mine, term, NT) for term in terms(shares, 2))
    for idx in range(HEADS):
        out = jnp.zeros((TOK, HD), F32)
        for peer in range(SIDE):
            col = HEADS * peer + idx
            out += all_ref[peer, :TOK, head(idx)].astype(F32) * shares[:, col : col + 1]
        att_ref[:, head(idx)] = out.astype(BF16)


def backward_body(ready, done, quad_ref, q_ref, kv_ref, grad_ref, norm_ref, dkv_ref, dq_ref):
    for idx in range(HEADS):
        ready(1, idx)
        ready(2, idx)
        ready(2, HEADS + idx)
        ready(3, idx)
        keys = kv_ref[:, head(idx)]
        keys_t = keys.T
        values = kv_ref[:, head(HEADS + idx)]
        d_keys = jnp.zeros((TILE, HD), F32)
        d_values = jnp.zeros((TILE, HD), F32)
        for start in range(0, TILE, QB):
            cols = slice(start, start + QB)
            query = q_ref[cols, head(idx)]
            grad = grad_ref[cols, head(idx)]
            scores = dot(keys, query, NT) * SCALE
            weights = jnp.exp2((scores - norm_ref[idx : idx + 1, cols]) * LOG2E)
            d_probs = dot(values, grad, NT)
            d_scores = weights * (d_probs - norm_ref[HEADS + idx : HEADS + idx + 1, cols])
            d_scores = d_scores.astype(BF16)
            d_values += dot(weights.astype(BF16), grad)
            d_keys += dot(d_scores, query)
            dq_ref[cols, head(idx)] = (dot(keys_t, d_scores) * SCALE).T.astype(BF16)
        dkv_ref[:, head(idx)] = (d_keys * SCALE).astype(BF16)
        dkv_ref[:, head(HEADS + idx)] = d_values.astype(BF16)
        done(0, idx)
        done(0, HEADS + idx)


def output_body(sorted_ref, w_ref, row_ref, part_ref):
    order, _ = sorted_by_block(row_ref[...])
    attended = dot(order, sorted_ref[...], TN).astype(BF16)
    for part in range(4):
        part_ref[part] = dot(attended, w_ref[:, part * SPAN : (part + 1) * SPAN]).astype(BF16)


def weight_body(both_ref, out_ref):
    total = jnp.zeros((COLS, COLS), F32)
    for peer in range(SIDE):
        total += dot(both_ref[peer, :, COLS:], both_ref[peer, :, :COLS], TN)
    out_ref[...] = total.astype(BF16)


def shift(value, axis, step, size):
    return lax.ppermute(value, axis, [(i, (i + step) % size) for i in range(size)])


def exchange(value, axis):
    return lax.all_to_all(value, axis, split_axis=0, concat_axis=0, tiled=True)


def gather_quad(value):
    return exchange(jnp.tile(value, (SIDE, 1)), QUAD)


def scatter_quad(blocks):
    return [blocks[0]] + [shift(blocks[step], QUAD, step, SIDE) for step in range(1, SIDE)]


def pick(value, idx, axis):
    return lax.dynamic_index_in_dim(value, idx, axis, keepdims=False)


def together(*values):
    return lax.optimization_barrier(values)


def on_device(main_hidden, ctrl_query, ctrl_key, ctrl_value, w_out, d_mixed, control_slot):
    y_pos, core = lax.axis_index("yh"), lax.axis_index("co")
    quad = lax.axis_index("x") * 2 + lax.axis_index("yl")
    slot_row = control_slot.reshape(1, TOK)
    y_one, core_one, quad_one = (p.reshape(1).astype(jnp.int32) for p in (y_pos, core, quad))

    key_value = jnp.concatenate([ctrl_key, ctrl_value], axis=1)
    key_value = lax.all_gather(key_value, "z", axis=0, tiled=True)
    along = shift(d_mixed, "yh", 1, 2)
    across = shift(d_mixed, "co", 1, 2)
    query = jnp.tile(ctrl_query, (SIDE, 1))
    query, along, across = together(query, along, across)
    query = exchange(query, QUAD)
    both = shift(along, "co", 1, 2)
    payload, cuts = call(
        project_body,
        [far(((TOK, COLS + HD), BF16)), far(((SIDE, TOK, COLS), BF16))],
        y_one,
        core_one,
        far(d_mixed),
        far(along),
        far(across),
        far(both),
        far(w_out),
        slot_row,
        mib=16,
    )
    payload, query = together(payload, query)
    payload = exchange(payload, "z")
    arrived = gather_quad(payload)
    out_t, lse = call(
        forward_body,
        [((COLS, TILE), BF16), ((SIDE, TILE), F32)],
        far(query, HEADS),
        far(key_value, 2 * HEADS),
        mib=20,
    )
    grad, send = call(
        delta_body,
        [far(((TILE, COLS), BF16), HEADS), far(((SIDE, SLAB, COLS), BF16))],
        arrived,
        out_t,
        lse,
        mib=24,
    )
    norms, attended = call(
        merge_body,
        [((SIDE, TILE), F32), far(((TOK, COLS), BF16))],
        quad_one,
        exchange(send, QUAD),
        arrived,
        mib=16,
    )
    d_key_value, *d_query = call(
        backward_body,
        [far(((TILE, 2 * COLS), BF16), 2 * HEADS)],
        quad_one,
        far(query, HEADS),
        far(key_value, 2 * HEADS),
        far(grad, HEADS),
        norms,
        mib=24,
        stack=COLS,
    )
    attended = exchange(attended, "z")
    d_key_value, attended = together(d_key_value, attended)
    d_key_value = lax.psum_scatter(d_key_value, "z", scatter_dimension=0, tiled=True)
    spread = jnp.broadcast_to(attended[None], (SIDE, TOK, COLS))
    spread = jnp.concatenate([spread, cuts], axis=2)
    spread, attended = together(spread, attended)
    gathered = exchange(spread, QUAD)
    (partial_out,) = call(
        output_body,
        [((4, TOK, SPAN), BF16)],
        attended,
        w_out,
        slot_row,
        mib=16,
    )

    by_core = partial_out.reshape(2, 2, TOK, SPAN)
    summed = pick(by_core, core, 1).astype(F32) + shift(
        pick(by_core, 1 - core, 1), "co", 1, 2
    ).astype(F32)
    residual = pick(summed, y_pos, 0) + shift(
        pick(summed, 1 - y_pos, 0).astype(BF16), "yh", 1, 2
    ).astype(F32)
    main_mixed = (main_hidden.astype(F32) + residual).astype(BF16)

    (d_w_out,) = call(
        weight_body,
        [far(((COLS, COLS), BF16))],
        gathered,
        mib=16,
    )
    d_w_out, *d_query = together(d_w_out, *d_query)
    d_query = sum(block.astype(F32) for block in scatter_quad(d_query))
    d_w_out = exchange(d_w_out, "z").reshape(SIDE, COLS // SIDE, COLS)
    d_w_out = jnp.sum(d_w_out.astype(F32), axis=0).T
    return (
        main_mixed,
        d_query.astype(BF16),
        d_key_value[:, :COLS],
        d_key_value[:, COLS:],
        d_w_out,
    )


def solution(mesh):
    fine = Mesh(mesh.devices.reshape(2, 2, 4, 2, 8), ("yh", "co", "x", "yl", "z"))
    grp, blk = ("yh", "co"), ("x", "yl", "z")
    in_specs = (
        P(blk, grp),
        P(blk, grp),
        P(blk, grp),
        P(blk, grp),
        P(grp, None),
        P(blk, grp),
        P(blk),
    )
    out_specs = (
        P(blk, grp),
        P(blk, grp),
        P(blk, grp),
        P(blk, grp),
        P(grp, blk),
    )
    return jax.shard_map(
        on_device, mesh=fine, in_specs=in_specs, out_specs=out_specs, check_vma=False
    )
```

```python
import math

import jax
import jax.numpy as jnp
from jax import lax
from jax.experimental import pallas as pl
from jax.experimental.pallas import tpu as pltpu
from jax.sharding import Mesh
from jax.sharding import PartitionSpec as P

HD = 128
HEADS = 3
COLS = HEADS * HD
TOK = 128
SIDE = 8
TILE = TOK * SIDE
QB = 256
QF = 1024
SCALE = 1.0 / math.sqrt(HD)
LOG2E = math.log2(math.e)
PEER = TOK // SIDE
SPAN = 768
QUAD = ("x", "yl")
F32 = jnp.float32
BF16 = jnp.bfloat16
NT = (((1,), (1,)), ((), ()))
TN = (((0,), (0,)), ((), ()))
HBM = pl.BlockSpec(memory_space=pltpu.HBM)
VMEM = pl.BlockSpec(memory_space=pltpu.VMEM)
SMEM = pl.BlockSpec(memory_space=pltpu.SMEM)
MIB = 1024 * 1024
STAT = 16
SLAB = TOK + 3 * STAT


def dot(left, right, dims=(((1,), (0,)), ((), ()))):
    return lax.dot_general(left, right, dims, preferred_element_type=F32)


def far(array, parts=1):
    return array, parts


def block_copies(source, dest, sems, first, parts):
    width = source.shape[-1] // parts
    found = []
    for n in range(parts):
        here, there = source, dest
        if parts > 1:
            here, there = (r.at[:, n * width : (n + 1) * width] for r in (source, dest))
        found.append(pltpu.make_async_copy(here, there, sems.at[first + n]))
    return found


def call(body, out, *args, mib, stack=None):
    arg_parts = [arg[1] if isinstance(arg, tuple) else 0 for arg in args]
    args = [arg[0] if isinstance(arg, tuple) else arg for arg in args]
    out_parts = [one[1] if isinstance(one[1], int) else 0 for one in out]
    out = [one[0] if isinstance(one[1], int) else one for one in out]
    n_in, n_out = len(args), len(out)
    far_in = [i for i in range(n_in) if arg_parts[i]]
    far_out = [i for i in range(n_out) if out_parts[i]]
    n_load, n_store = sum(arg_parts), sum(out_parts)

    def kernel(*refs):
        ins, outs = list(refs[:n_in]), list(refs[n_in : n_in + n_out])
        rest = list(refs[n_in + n_out :])
        if stack:
            pieces, rest = rest[:SIDE], rest[SIDE:]
            piece_sem, whole = rest.pop(), rest.pop()
            outs.append(whole)
        loads, stores = {}, {}
        load_sem = rest.pop(0) if n_load else None
        store_sem = rest.pop(0) if n_store else None
        first = 0
        for i in far_in:
            spot = rest.pop(0)
            loads[i] = block_copies(ins[i], spot, load_sem, first, arg_parts[i])
            first += arg_parts[i]
            ins[i] = spot
        first = 0
        for i in far_out:
            spot = rest.pop(0)
            stores[i] = block_copies(spot, outs[i], store_sem, first, out_parts[i])
            first += out_parts[i]
            outs[i] = spot
        for n in range(max(arg_parts)):
            for i in far_in:
                if n < arg_parts[i]:
                    loads[i][n].start()
        for i in far_in:
            if arg_parts[i] == 1:
                loads[i][0].wait()
        started = set()

        def ready(i, n):
            loads[i][n].wait()

        def done(i, n):
            stores[i][n].start()
            started.add((i, n))

        steps = (ready, done) if max(arg_parts) > 1 or max(out_parts) > 1 else ()
        body(*steps, *ins, *outs, *rest)
        for i in far_out:
            for n in range(out_parts[i]):
                if (i, n) not in started:
                    stores[i][n].start()
        if stack:
            stores[n_out] = [
                pltpu.make_async_copy(
                    whole.at[rows_of(around(ins[0][0], step)), :], piece, piece_sem.at[step]
                )
                for step, piece in enumerate(pieces)
            ]
            for copy in stores[n_out]:
                copy.start()
        for i in stores:
            for copy in stores[i]:
                copy.wait()

    dma = pltpu.SemaphoreType.DMA
    return pl.pallas_call(
        kernel,
        out_shape=[
            pltpu.HBM(*one) if out_parts[i] else jax.ShapeDtypeStruct(*one)
            for i, one in enumerate(out)
        ]
        + ([pltpu.HBM((TOK, stack), BF16)] * SIDE if stack else []),
        in_specs=[
            HBM if arg_parts[i] else SMEM if args[i].shape == (1,) else VMEM for i in range(n_in)
        ],
        out_specs=[HBM if parts else VMEM for parts in out_parts] + ([HBM] * SIDE if stack else []),
        scratch_shapes=[
            *([dma((n_load,))] if n_load else []),
            *([dma((n_store,))] if n_store else []),
            *[pltpu.VMEM(args[i].shape, args[i].dtype) for i in far_in],
            *[pltpu.VMEM(*out[i]) for i in far_out],
            *([pltpu.VMEM((TILE, stack), BF16), dma((SIDE,))] if stack else []),
        ],
        compiler_params=pltpu.CompilerParams(vmem_limit_bytes=mib * MIB),
    )(
        *[
            pltpu.with_memory_space_constraint(arg, pltpu.HBM) if arg_parts[i] else arg
            for i, arg in enumerate(args)
        ]
    )


def around(pos, step):
    return lax.rem(pos + (step + SIDE), SIDE)


def rows_of(pos):
    return pl.ds(pl.multiple_of(pos * TOK, TOK), TOK)


def head(idx):
    return slice(idx * HD, (idx + 1) * HD)


def block_of(slot):
    return (slot >> 7) & (SIDE - 1)


def sorted_by_block(slot_row):
    first = lax.broadcasted_iota(jnp.int32, (TOK, TOK), 0)
    second = lax.broadcasted_iota(jnp.int32, (TOK, TOK), 1)
    spread = jnp.where(first == second, slot_row.astype(F32), 0.0)
    slot_col = jnp.sum(spread, axis=1, keepdims=True).astype(jnp.int32)
    same = (block_of(slot_row) == block_of(slot_col)) & (first < second)
    ahead = jnp.sum(jnp.where(same, 1.0, 0.0), axis=0, keepdims=True).astype(jnp.int32)
    rank = block_of(slot_row) * PEER + ahead
    order = jnp.where(first == rank, 1.0, 0.0).astype(BF16)
    place = jnp.where(
        second == 0,
        (slot_col >> 10).astype(F32),
        jnp.where(second == 1, (slot_col & (TOK - 1)).astype(F32), 0.0),
    )
    return order, place


def project_body(
    y_ref, core_ref, d0_ref, d1_ref, d2_ref, d3_ref, w_ref, row_ref, pay_ref
):
    y_pos, core = y_ref[0], core_ref[0]
    order, place = sorted_by_block(row_ref[...])
    total = jnp.zeros((TOK, COLS), F32)
    pieces = (
        (d0_ref, y_pos, core),
        (d1_ref, 1 - y_pos, core),
        (d2_ref, y_pos, 1 - core),
        (d3_ref, 1 - y_pos, 1 - core),
    )
    for d_ref, along, across in pieces:
        part = 2 * along + across
        here = pl.ds(pl.multiple_of(part * SPAN, SPAN), SPAN)
        total += dot(d_ref[...], w_ref[:, here], NT)
    pay_ref[:, :COLS] = dot(order, total.astype(BF16)).astype(BF16)
    pay_ref[:, COLS:] = dot(order, place.astype(BF16)).astype(BF16)


def cut_body(y_ref, core_ref, d0_ref, d1_ref, d2_ref, d3_ref, row_ref, cut_ref):
    order, _ = sorted_by_block(row_ref[...])
    y_pos, core = y_ref[0], core_ref[0]
    pieces = (
        (d0_ref, y_pos, core),
        (d1_ref, 1 - y_pos, core),
        (d2_ref, y_pos, 1 - core),
        (d3_ref, 1 - y_pos, 1 - core),
    )
    for d_ref, along, across in pieces:
        part = 2 * along + across
        rows = dot(order, d_ref[...]).astype(BF16)
        cut_ref[2 * part, :, COLS:] = rows[:, :COLS]
        cut_ref[2 * part + 1, :, COLS:] = rows[:, COLS:]


def forward_body(ready, done, quad_ref, kv_ref, *rest):
    blocks, (q_ref, out_ref, lse_ref) = rest[:-3], rest[-3:]
    for step, block_ref in enumerate(blocks):
        q_ref[rows_of(around(quad_ref[0], -step)), :] = block_ref[...]
    for idx in range(HEADS):
        done(0, idx)
    lse_ref[...] = jnp.zeros_like(lse_ref)
    for idx in range(HEADS):
        ready(1, idx)
        ready(1, HEADS + idx)
        keys = kv_ref[:, head(idx)]
        values_t = kv_ref[:, head(HEADS + idx)].T
        for start in range(0, TILE, QF):
            cols = slice(start, start + QF)
            scores = dot(keys, q_ref[cols, head(idx)], NT)
            peak = jnp.max(scores, axis=0, keepdims=True)
            weights = jnp.exp2((scores - peak) * (SCALE * LOG2E))
            total = jnp.sum(weights, axis=0, keepdims=True)
            out_ref[head(idx), cols] = (dot(values_t, weights.astype(BF16)) / total).astype(BF16)
            lse_ref[idx : idx + 1, cols] = peak * SCALE + jnp.log(total)


def places(arrived):
    place = arrived.astype(F32)
    target = place[:, 0:1] * float(TOK) + place[:, 1:2]
    lanes = lax.broadcasted_iota(jnp.int32, (place.shape[0], TILE), 1)
    return jnp.where(lanes == target.astype(jnp.int32), 1.0, 0.0).astype(BF16)


def terms(value, count):
    found = []
    for _ in range(count):
        found.append(value.astype(BF16))
        value = value - found[-1].astype(F32)
    return found


def delta_body(ready, done, arrived_ref, out_ref, lse_ref, grad_ref, send_ref):
    order = places(arrived_ref[:, COLS:])
    deltas = []
    for idx in range(HEADS):
        grad_t = dot(arrived_ref[:, head(idx)].T, order)
        grad_ref[:, head(idx)] = grad_t.T.astype(BF16)
        done(0, idx)
        deltas.append(jnp.sum(grad_t * out_ref[head(idx), :].astype(F32), axis=0, keepdims=True))
        rows = dot(out_ref[head(idx), :], order, NT).T.astype(BF16)
        for peer in range(SIDE):
            send_ref[peer, :TOK, head(idx)] = rows[peer * TOK : (peer + 1) * TOK]
    zero = jnp.zeros((1, TILE), BF16)
    stats = [t for t in terms(lse_ref[:HEADS, :], 3)]
    stats += terms(jnp.concatenate(deltas, axis=0), 2)
    stats = jnp.concatenate([t.astype(F32) for t in stats] + [zero.astype(F32)], axis=0).astype(BF16)
    for peer in range(SIDE):
        for n, start in enumerate(range(0, TILE, COLS)):
            width = min(COLS, TILE - start)
            send_ref[peer, TOK + STAT * n : TOK + STAT * (n + 1), :width] = stats[:, start : start + width]


def merge_body(quad_ref, all_ref, arrived_ref, norm_ref, att_ref):
    lses, deltas = [], []
    for peer in range(SIDE):
        parts = []
        for n, start in enumerate(range(0, TILE, COLS)):
            width = min(COLS, TILE - start)
            parts.append(all_ref[peer, TOK + STAT * n : TOK + STAT * (n + 1), :width].astype(F32))
        stats = jnp.concatenate(parts, axis=1)
        lses.append(stats[0:3] + stats[3:6] + stats[6:9])
        deltas.append(stats[9:12] + stats[12:15])
    peak = lses[0]
    for one in lses[1:]:
        peak = jnp.maximum(peak, one)
    weights = [jnp.exp(one - peak) for one in lses]
    total = sum(weights)
    norm_ref[...] = jnp.zeros_like(norm_ref)
    norm_ref[:HEADS, :] = peak + jnp.log(total)
    norm_ref[HEADS : 2 * HEADS, :] = sum(w * d for w, d in zip(weights, deltas)) / total
    shares = jnp.concatenate([w / total for w in weights], axis=0)
    mine = places(arrived_ref[rows_of(quad_ref[0]), COLS:])
    shares = sum(dot(mine, term, NT) for term in terms(shares, 2))
    for idx in range(HEADS):
        out = jnp.zeros((TOK, HD), F32)
        for peer in range(SIDE):
            col = HEADS * peer + idx
            out += all_ref[peer, :TOK, head(idx)].astype(F32) * shares[:, col : col + 1]
        att_ref[:, head(idx)] = out.astype(BF16)


def backward_body(ready, done, quad_ref, q_ref, kv_ref, grad_ref, norm_ref, dkv_ref, dq_ref):
    for idx in range(HEADS):
        ready(1, idx)
        ready(2, idx)
        ready(2, HEADS + idx)
        ready(3, idx)
        keys = kv_ref[:, head(idx)]
        keys_t = keys.T
        values = kv_ref[:, head(HEADS + idx)]
        d_keys = jnp.zeros((TILE, HD), F32)
        d_values = jnp.zeros((TILE, HD), F32)
        for start in range(0, TILE, QB):
            cols = slice(start, start + QB)
            query = q_ref[cols, head(idx)]
            grad = grad_ref[cols, head(idx)]
            scores = dot(keys, query, NT) * SCALE
            weights = jnp.exp2((scores - norm_ref[idx : idx + 1, cols]) * LOG2E)
            d_probs = dot(values, grad, NT)
            d_scores = weights * (d_probs - norm_ref[HEADS + idx : HEADS + idx + 1, cols])
            d_scores = d_scores.astype(BF16)
            d_values += dot(weights.astype(BF16), grad)
            d_keys += dot(d_scores, query)
            dq_ref[cols, head(idx)] = (dot(keys_t, d_scores) * SCALE).T.astype(BF16)
        dkv_ref[:, head(idx)] = (d_keys * SCALE).astype(BF16)
        dkv_ref[:, head(HEADS + idx)] = d_values.astype(BF16)
        done(0, idx)
        done(0, HEADS + idx)


def output_body(sorted_ref, w_ref, row_ref, part_ref):
    order, _ = sorted_by_block(row_ref[...])
    attended = dot(order, sorted_ref[...], TN).astype(BF16)
    for part in range(4):
        part_ref[part] = dot(attended, w_ref[:, part * SPAN : (part + 1) * SPAN]).astype(BF16)


def weight_body(both_ref, out_ref):
    total = jnp.zeros((COLS, COLS), F32)
    for peer in range(SIDE):
        total += dot(both_ref[peer, :, COLS:], both_ref[peer, :, :COLS], TN)
    out_ref[...] = total.astype(BF16)


def fill_spread(attended, spread):
    def kernel(att_ref, _, out_ref, held, load_sem, sems):
        load = pltpu.make_async_copy(att_ref, held, load_sem)
        load.start()
        load.wait()
        copies = [
            pltpu.make_async_copy(held, out_ref.at[peer, :, :COLS], sems.at[peer])
            for peer in range(SIDE)
        ]
        for copy in copies:
            copy.start()
        for copy in copies:
            copy.wait()

    return pl.pallas_call(
        kernel,
        out_shape=pltpu.HBM(spread.shape, spread.dtype),
        in_specs=[HBM, HBM],
        out_specs=HBM,
        input_output_aliases={1: 0},
        scratch_shapes=[
            pltpu.VMEM(attended.shape, attended.dtype),
            pltpu.SemaphoreType.DMA,
            pltpu.SemaphoreType.DMA((SIDE,)),
        ],
    )(*[pltpu.with_memory_space_constraint(arg, pltpu.HBM) for arg in (attended, spread)])


def shift(value, axis, step, size):
    return lax.ppermute(value, axis, [(i, (i + step) % size) for i in range(size)])


def exchange(value, axis):
    return lax.all_to_all(value, axis, split_axis=0, concat_axis=0, tiled=True)


def gather_quad(value):
    return exchange(jnp.tile(value, (SIDE, 1)), QUAD)


def scatter_quad(blocks):
    return [blocks[0]] + [shift(blocks[step], QUAD, step, SIDE) for step in range(1, SIDE)]


def pick(value, idx, axis):
    return lax.dynamic_index_in_dim(value, idx, axis, keepdims=False)


def together(*values):
    return lax.optimization_barrier(values)


def on_device(main_hidden, ctrl_query, ctrl_key, ctrl_value, w_out, d_mixed, control_slot):
    y_pos, core = lax.axis_index("yh"), lax.axis_index("co")
    quad = lax.axis_index("x") * 2 + lax.axis_index("yl")
    slot_row = control_slot.reshape(1, TOK)
    y_one, core_one, quad_one = (p.reshape(1).astype(jnp.int32) for p in (y_pos, core, quad))

    key_value = jnp.concatenate([ctrl_key, ctrl_value], axis=1)
    key_value = lax.all_gather(key_value, "z", axis=0, tiled=True)
    along = shift(d_mixed, "yh", 1, 2)
    across = shift(d_mixed, "co", 1, 2)
    both = shift(along, "co", 1, 2)
    (payload,) = call(
        project_body,
        [far(((TOK, COLS + HD), BF16))],
        y_one,
        core_one,
        far(d_mixed),
        far(along),
        far(across),
        far(both),
        far(w_out),
        slot_row,
        mib=16,
    )
    payload, ctrl_query = together(payload, ctrl_query)
    payload = exchange(payload, "z")
    query = scatter_quad([ctrl_query] * SIDE)
    payload, *query = together(payload, *query)
    arrived = gather_quad(payload)
    query, out_t, lse = call(
        forward_body,
        [far(((TILE, COLS), BF16), HEADS), ((COLS, TILE), BF16), ((SIDE, TILE), F32)],
        quad_one,
        far(key_value, 2 * HEADS),
        *[far(block) for block in query],
        mib=40,
    )
    grad, send = call(
        delta_body,
        [far(((TILE, COLS), BF16), HEADS), far(((SIDE, SLAB, COLS), BF16))],
        arrived,
        out_t,
        lse,
        mib=24,
    )
    stats = exchange(send, QUAD)
    send, *pieces = together(send, d_mixed, along, across, both)
    (spread,) = call(
        cut_body,
        [far(((SIDE, TOK, 2 * COLS), BF16))],
        y_one,
        core_one,
        *[far(piece) for piece in pieces],
        slot_row,
        mib=16,
    )
    stats, spread = together(stats, spread)
    norms, attended = call(
        merge_body,
        [((SIDE, TILE), F32), far(((TOK, COLS), BF16))],
        quad_one,
        stats,
        arrived,
        mib=16,
    )
    d_key_value, *d_query = call(
        backward_body,
        [far(((TILE, 2 * COLS), BF16), 2 * HEADS)],
        quad_one,
        far(query, HEADS),
        far(key_value, 2 * HEADS),
        far(grad, HEADS),
        norms,
        mib=24,
        stack=COLS,
    )
    attended = exchange(attended, "z")
    d_key_value, attended = together(d_key_value, attended)
    d_key_value = lax.psum_scatter(d_key_value, "z", scatter_dimension=0, tiled=True)
    spread = fill_spread(attended, spread)
    spread, attended, *d_query[1:4] = together(spread, attended, *d_query[1:4])
    gathered = exchange(spread, QUAD)
    (partial_out,) = call(
        output_body,
        [((4, TOK, SPAN), BF16)],
        attended,
        w_out,
        slot_row,
        mib=16,
    )

    by_core = partial_out.reshape(2, 2, TOK, SPAN)
    summed = pick(by_core, core, 1).astype(F32) + shift(
        pick(by_core, 1 - core, 1), "co", 1, 2
    ).astype(F32)
    half = pick(summed, 1 - y_pos, 0).astype(BF16)
    residual = pick(summed, y_pos, 0) + shift(half, "yh", 1, 2).astype(F32)
    main_mixed = (main_hidden.astype(F32) + residual).astype(BF16)

    (d_w_out,) = call(
        weight_body,
        [far(((COLS, COLS), BF16))],
        gathered,
        mib=16,
    )
    d_w_out, *d_query[4:] = together(d_w_out, *d_query[4:])
    d_query = sum(block.astype(F32) for block in scatter_quad(d_query))
    d_w_out = exchange(d_w_out, "z").reshape(SIDE, COLS // SIDE, COLS)
    d_key, d_value = d_key_value[:, :COLS], d_key_value[:, COLS:]
    d_w_out, d_key, d_value = together(d_w_out, d_key, d_value)
    d_w_out = jnp.sum(d_w_out.astype(F32), axis=0).T
    return (
        main_mixed,
        d_query.astype(BF16),
        d_key,
        d_value,
        d_w_out,
    )


def solution(mesh):
    fine = Mesh(mesh.devices.reshape(2, 2, 4, 2, 8), ("yh", "co", "x", "yl", "z"))
    grp, blk = ("yh", "co"), ("x", "yl", "z")
    in_specs = (
        P(blk, grp),
        P(blk, grp),
        P(blk, grp),
        P(blk, grp),
        P(grp, None),
        P(blk, grp),
        P(blk),
    )
    out_specs = (
        P(blk, grp),
        P(blk, grp),
        P(blk, grp),
        P(blk, grp),
        P(grp, blk),
    )
    return jax.shard_map(
        on_device, mesh=fine, in_specs=in_specs, out_specs=out_specs, check_vma=False
    )
```

```python
import math

import jax
import jax.numpy as jnp
from jax import lax
from jax.experimental import pallas as pl
from jax.experimental.pallas import tpu as pltpu
from jax.sharding import Mesh
from jax.sharding import PartitionSpec as P

HD = 128
HEADS = 3
COLS = HEADS * HD
TOK = 128
SIDE = 8
TILE = TOK * SIDE
QB = 256
QF = 1024
SCALE = 1.0 / math.sqrt(HD)
LOG2E = math.log2(math.e)
PEER = TOK // SIDE
SPAN = 768
QUAD = ("x", "yl")
F32 = jnp.float32
BF16 = jnp.bfloat16
NT = (((1,), (1,)), ((), ()))
TN = (((0,), (0,)), ((), ()))
HBM = pl.BlockSpec(memory_space=pltpu.HBM)
VMEM = pl.BlockSpec(memory_space=pltpu.VMEM)
SMEM = pl.BlockSpec(memory_space=pltpu.SMEM)
MIB = 1024 * 1024
STAT = 16
SLAB = TOK + 3 * STAT


def dot(left, right, dims=(((1,), (0,)), ((), ()))):
    return lax.dot_general(left, right, dims, preferred_element_type=F32)


def far(array, parts=1):
    return array, parts


def block_copies(source, dest, sems, first, parts):
    width = source.shape[-1] // parts
    found = []
    for n in range(parts):
        here, there = source, dest
        if parts > 1:
            here, there = (r.at[:, n * width : (n + 1) * width] for r in (source, dest))
        found.append(pltpu.make_async_copy(here, there, sems.at[first + n]))
    return found


def call(body, out, *args, mib, stack=None):
    arg_parts = [arg[1] if isinstance(arg, tuple) else 0 for arg in args]
    args = [arg[0] if isinstance(arg, tuple) else arg for arg in args]
    out_parts = [one[1] if isinstance(one[1], int) else 0 for one in out]
    out = [one[0] if isinstance(one[1], int) else one for one in out]
    n_in, n_out = len(args), len(out)
    far_in = [i for i in range(n_in) if arg_parts[i]]
    far_out = [i for i in range(n_out) if out_parts[i]]
    n_load, n_store = sum(arg_parts), sum(out_parts)

    def kernel(*refs):
        ins, outs = list(refs[:n_in]), list(refs[n_in : n_in + n_out])
        rest = list(refs[n_in + n_out :])
        if stack:
            pieces, rest = rest[:SIDE], rest[SIDE:]
            piece_sem, whole = rest.pop(), rest.pop()
            outs.append(whole)
        loads, stores = {}, {}
        load_sem = rest.pop(0) if n_load else None
        store_sem = rest.pop(0) if n_store else None
        first = 0
        for i in far_in:
            spot = rest.pop(0)
            loads[i] = block_copies(ins[i], spot, load_sem, first, arg_parts[i])
            first += arg_parts[i]
            ins[i] = spot
        first = 0
        for i in far_out:
            spot = rest.pop(0)
            stores[i] = block_copies(spot, outs[i], store_sem, first, out_parts[i])
            first += out_parts[i]
            outs[i] = spot
        for n in range(max(arg_parts)):
            for i in far_in:
                if n < arg_parts[i]:
                    loads[i][n].start()
        for i in far_in:
            if arg_parts[i] == 1:
                loads[i][0].wait()
        started = set()

        def ready(i, n):
            loads[i][n].wait()

        def done(i, n):
            stores[i][n].start()
            started.add((i, n))

        steps = (ready, done) if max(arg_parts) > 1 or max(out_parts) > 1 else ()
        body(*steps, *ins, *outs, *rest)
        for i in far_out:
            for n in range(out_parts[i]):
                if (i, n) not in started:
                    stores[i][n].start()
        if stack:
            stores[n_out] = [
                pltpu.make_async_copy(
                    whole.at[rows_of(around(ins[0][0], step)), :], piece, piece_sem.at[step]
                )
                for step, piece in enumerate(pieces)
            ]
            for copy in stores[n_out]:
                copy.start()
        for i in stores:
            for copy in stores[i]:
                copy.wait()

    dma = pltpu.SemaphoreType.DMA
    return pl.pallas_call(
        kernel,
        out_shape=[
            pltpu.HBM(*one) if out_parts[i] else jax.ShapeDtypeStruct(*one)
            for i, one in enumerate(out)
        ]
        + ([pltpu.HBM((TOK, stack), BF16)] * SIDE if stack else []),
        in_specs=[
            HBM if arg_parts[i] else SMEM if args[i].shape == (1,) else VMEM for i in range(n_in)
        ],
        out_specs=[HBM if parts else VMEM for parts in out_parts] + ([HBM] * SIDE if stack else []),
        scratch_shapes=[
            *([dma((n_load,))] if n_load else []),
            *([dma((n_store,))] if n_store else []),
            *[pltpu.VMEM(args[i].shape, args[i].dtype) for i in far_in],
            *[pltpu.VMEM(*out[i]) for i in far_out],
            *([pltpu.VMEM((TILE, stack), BF16), dma((SIDE,))] if stack else []),
        ],
        compiler_params=pltpu.CompilerParams(vmem_limit_bytes=mib * MIB),
    )(
        *[
            pltpu.with_memory_space_constraint(arg, pltpu.HBM) if arg_parts[i] else arg
            for i, arg in enumerate(args)
        ]
    )


def around(pos, step):
    return lax.rem(pos + (step + SIDE), SIDE)


def rows_of(pos):
    return pl.ds(pl.multiple_of(pos * TOK, TOK), TOK)


def head(idx):
    return slice(idx * HD, (idx + 1) * HD)


def block_of(slot):
    return (slot >> 7) & (SIDE - 1)


def sorted_by_block(slot_row):
    first = lax.broadcasted_iota(jnp.int32, (TOK, TOK), 0)
    second = lax.broadcasted_iota(jnp.int32, (TOK, TOK), 1)
    spread = jnp.where(first == second, slot_row.astype(F32), 0.0)
    slot_col = jnp.sum(spread, axis=1, keepdims=True).astype(jnp.int32)
    same = (block_of(slot_row) == block_of(slot_col)) & (first < second)
    ahead = jnp.sum(jnp.where(same, 1.0, 0.0), axis=0, keepdims=True).astype(jnp.int32)
    rank = block_of(slot_row) * PEER + ahead
    order = jnp.where(first == rank, 1.0, 0.0).astype(BF16)
    place = jnp.where(
        second == 0,
        (slot_col >> 10).astype(F32),
        jnp.where(second == 1, (slot_col & (TOK - 1)).astype(F32), 0.0),
    )
    return order, place


def project_body(
    y_ref, core_ref, d0_ref, d1_ref, d2_ref, d3_ref, w_ref, row_ref, pay_ref
):
    y_pos, core = y_ref[0], core_ref[0]
    order, place = sorted_by_block(row_ref[...])
    total = jnp.zeros((TOK, COLS), F32)
    pieces = (
        (d0_ref, y_pos, core),
        (d1_ref, 1 - y_pos, core),
        (d2_ref, y_pos, 1 - core),
        (d3_ref, 1 - y_pos, 1 - core),
    )
    for d_ref, along, across in pieces:
        part = 2 * along + across
        here = pl.ds(pl.multiple_of(part * SPAN, SPAN), SPAN)
        total += dot(d_ref[...], w_ref[:, here], NT)
    pay_ref[:, :COLS] = dot(order, total.astype(BF16)).astype(BF16)
    pay_ref[:, COLS:] = dot(order, place.astype(BF16)).astype(BF16)


def cut_body(y_ref, core_ref, d0_ref, d1_ref, d2_ref, d3_ref, row_ref, cut_ref):
    order, _ = sorted_by_block(row_ref[...])
    y_pos, core = y_ref[0], core_ref[0]
    pieces = (
        (d0_ref, y_pos, core),
        (d1_ref, 1 - y_pos, core),
        (d2_ref, y_pos, 1 - core),
        (d3_ref, 1 - y_pos, 1 - core),
    )
    for d_ref, along, across in pieces:
        part = 2 * along + across
        rows = dot(order, d_ref[...]).astype(BF16)
        cut_ref[2 * part, :, COLS:] = rows[:, :COLS]
        cut_ref[2 * part + 1, :, COLS:] = rows[:, COLS:]


def forward_body(ready, done, quad_ref, kv_ref, *rest):
    blocks, (q_ref, out_ref, lse_ref) = rest[:-3], rest[-3:]
    for step, block_ref in enumerate(blocks):
        q_ref[rows_of(around(quad_ref[0], -step)), :] = block_ref[...]
    for idx in range(HEADS):
        done(0, idx)
    lse_ref[...] = jnp.zeros_like(lse_ref)
    for idx in range(HEADS):
        ready(1, idx)
        ready(1, HEADS + idx)
        keys = kv_ref[:, head(idx)]
        values_t = kv_ref[:, head(HEADS + idx)].T
        for start in range(0, TILE, QF):
            cols = slice(start, start + QF)
            scores = dot(keys, q_ref[cols, head(idx)], NT)
            peak = jnp.max(scores, axis=0, keepdims=True)
            weights = jnp.exp2((scores - peak) * (SCALE * LOG2E))
            total = jnp.sum(weights, axis=0, keepdims=True)
            out_ref[head(idx), cols] = (dot(values_t, weights.astype(BF16)) / total).astype(BF16)
            lse_ref[idx : idx + 1, cols] = peak * SCALE + jnp.log(total)


def places(arrived):
    place = arrived.astype(F32)
    target = place[:, 0:1] * float(TOK) + place[:, 1:2]
    lanes = lax.broadcasted_iota(jnp.int32, (place.shape[0], TILE), 1)
    return jnp.where(lanes == target.astype(jnp.int32), 1.0, 0.0).astype(BF16)


def terms(value, count):
    found = []
    for _ in range(count):
        found.append(value.astype(BF16))
        value = value - found[-1].astype(F32)
    return found


def delta_body(ready, done, arrived_ref, out_ref, lse_ref, grad_ref, send_ref):
    order = places(arrived_ref[:, COLS:])
    deltas = []
    for idx in range(HEADS):
        grad_t = dot(arrived_ref[:, head(idx)].T, order)
        grad_ref[:, head(idx)] = grad_t.T.astype(BF16)
        done(0, idx)
        deltas.append(jnp.sum(grad_t * out_ref[head(idx), :].astype(F32), axis=0, keepdims=True))
        rows = dot(out_ref[head(idx), :], order, NT).T.astype(BF16)
        for peer in range(SIDE):
            send_ref[peer, :TOK, head(idx)] = rows[peer * TOK : (peer + 1) * TOK]
    zero = jnp.zeros((1, TILE), BF16)
    stats = [t for t in terms(lse_ref[:HEADS, :], 3)]
    stats += terms(jnp.concatenate(deltas, axis=0), 2)
    stats = jnp.concatenate([t.astype(F32) for t in stats] + [zero.astype(F32)], axis=0).astype(BF16)
    for peer in range(SIDE):
        for n, start in enumerate(range(0, TILE, COLS)):
            width = min(COLS, TILE - start)
            send_ref[peer, TOK + STAT * n : TOK + STAT * (n + 1), :width] = stats[:, start : start + width]


def merge_body(quad_ref, all_ref, arrived_ref, norm_ref, att_ref):
    lses, deltas = [], []
    for peer in range(SIDE):
        parts = []
        for n, start in enumerate(range(0, TILE, COLS)):
            width = min(COLS, TILE - start)
            parts.append(all_ref[peer, TOK + STAT * n : TOK + STAT * (n + 1), :width].astype(F32))
        stats = jnp.concatenate(parts, axis=1)
        lses.append(stats[0:3] + stats[3:6] + stats[6:9])
        deltas.append(stats[9:12] + stats[12:15])
    peak = lses[0]
    for one in lses[1:]:
        peak = jnp.maximum(peak, one)
    weights = [jnp.exp(one - peak) for one in lses]
    total = sum(weights)
    norm_ref[...] = jnp.zeros_like(norm_ref)
    norm_ref[:HEADS, :] = peak + jnp.log(total)
    norm_ref[HEADS : 2 * HEADS, :] = sum(w * d for w, d in zip(weights, deltas)) / total
    shares = jnp.concatenate([w / total for w in weights], axis=0)
    mine = places(arrived_ref[rows_of(quad_ref[0]), COLS:])
    shares = sum(dot(mine, term, NT) for term in terms(shares, 2))
    for idx in range(HEADS):
        out = jnp.zeros((TOK, HD), F32)
        for peer in range(SIDE):
            col = HEADS * peer + idx
            out += all_ref[peer, :TOK, head(idx)].astype(F32) * shares[:, col : col + 1]
        att_ref[:, head(idx)] = out.astype(BF16)


def backward_body(ready, done, quad_ref, q_ref, kv_ref, grad_ref, norm_ref, dkv_ref, dq_ref):
    for idx in range(HEADS):
        ready(1, idx)
        ready(2, idx)
        ready(2, HEADS + idx)
        ready(3, idx)
        keys = kv_ref[:, head(idx)]
        keys_t = keys.T
        values = kv_ref[:, head(HEADS + idx)]
        d_keys = jnp.zeros((TILE, HD), F32)
        d_values = jnp.zeros((TILE, HD), F32)
        for start in range(0, TILE, QB):
            cols = slice(start, start + QB)
            query = q_ref[cols, head(idx)]
            grad = grad_ref[cols, head(idx)]
            scores = dot(keys, query, NT) * SCALE
            weights = jnp.exp2((scores - norm_ref[idx : idx + 1, cols]) * LOG2E)
            d_probs = dot(values, grad, NT)
            d_scores = weights * (d_probs - norm_ref[HEADS + idx : HEADS + idx + 1, cols])
            d_scores = d_scores.astype(BF16)
            d_values += dot(weights.astype(BF16), grad)
            d_keys += dot(d_scores, query)
            dq_ref[cols, head(idx)] = (dot(keys_t, d_scores) * SCALE).T.astype(BF16)
        d_keys = (d_keys * SCALE).astype(BF16)
        d_values = d_values.astype(BF16)
        for peer in range(SIDE):
            rows = slice(peer * TOK, (peer + 1) * TOK)
            first = 2 * peer * TOK
            dkv_ref[first : first + TOK, head(idx)] = d_keys[rows]
            dkv_ref[first + TOK : first + 2 * TOK, head(idx)] = d_values[rows]
        done(0, idx)


def output_body(sorted_ref, w_ref, row_ref, part_ref):
    order, _ = sorted_by_block(row_ref[...])
    attended = dot(order, sorted_ref[...], TN).astype(BF16)
    for part in range(4):
        part_ref[part] = dot(attended, w_ref[:, part * SPAN : (part + 1) * SPAN]).astype(BF16)


def weight_body(both_ref, out_ref):
    both = both_ref[...].reshape(TILE, 2 * COLS)
    total = dot(both[:, COLS:], both[:, :COLS], TN)
    out_ref[...] = total.astype(BF16)


def fill_spread(attended, spread):
    def kernel(held, _, out_ref, sems):
        copies = [
            pltpu.make_async_copy(held, out_ref.at[peer, :, :COLS], sems.at[peer])
            for peer in range(SIDE)
        ]
        for copy in copies:
            copy.start()
        for copy in copies:
            copy.wait()

    return pl.pallas_call(
        kernel,
        out_shape=pltpu.HBM(spread.shape, spread.dtype),
        in_specs=[VMEM, HBM],
        out_specs=HBM,
        input_output_aliases={1: 0},
        scratch_shapes=[pltpu.SemaphoreType.DMA((SIDE,))],
    )(attended, pltpu.with_memory_space_constraint(spread, pltpu.HBM))


def shift(value, axis, step, size):
    return lax.ppermute(value, axis, [(i, (i + step) % size) for i in range(size)])


def exchange(value, axis):
    return lax.all_to_all(value, axis, split_axis=0, concat_axis=0, tiled=True)


def scatter_quad(blocks):
    return [blocks[0]] + [shift(blocks[step], QUAD, step, SIDE) for step in range(1, SIDE)]


def pick(value, idx, axis):
    return lax.dynamic_index_in_dim(value, idx, axis, keepdims=False)


def together(*values):
    return lax.optimization_barrier(values)


def on_device(main_hidden, ctrl_query, ctrl_key, ctrl_value, w_out, d_mixed, control_slot):
    y_pos, core = lax.axis_index("yh"), lax.axis_index("co")
    quad = lax.axis_index("x") * 2 + lax.axis_index("yl")
    slot_row = control_slot.reshape(1, TOK)
    y_one, core_one, quad_one = (p.reshape(1).astype(jnp.int32) for p in (y_pos, core, quad))

    key_value = jnp.concatenate([ctrl_key, ctrl_value], axis=1)
    key_value = lax.all_gather(key_value, "z", axis=0, tiled=True)
    along = shift(d_mixed, "yh", 1, 2)
    across = shift(d_mixed, "co", 1, 2)
    both = shift(along, "co", 1, 2)
    (payload,) = call(
        project_body,
        [far(((TOK, COLS + HD), BF16))],
        y_one,
        core_one,
        far(d_mixed),
        along,
        across,
        both,
        far(w_out),
        slot_row,
        mib=16,
    )
    payload, ctrl_query = together(payload, ctrl_query)
    payload = exchange(payload, "z")
    query = scatter_quad([ctrl_query] * SIDE)
    payload, *query = together(jnp.tile(payload, (SIDE, 1)), *query)
    arrived = exchange(payload, QUAD)
    query, out_t, lse = call(
        forward_body,
        [far(((TILE, COLS), BF16), HEADS), ((COLS, TILE), BF16), ((SIDE, TILE), F32)],
        quad_one,
        far(key_value, 2 * HEADS),
        *[far(block) for block in query],
        mib=40,
    )
    grad, send = call(
        delta_body,
        [far(((TILE, COLS), BF16), HEADS), far(((SIDE, SLAB, COLS), BF16))],
        arrived,
        out_t,
        lse,
        mib=24,
    )
    stats = exchange(send, QUAD)
    send, *pieces = together(send, d_mixed, along, across, both)
    (spread,) = call(
        cut_body,
        [far(((SIDE, TOK, 2 * COLS), BF16))],
        y_one,
        core_one,
        *[far(piece) for piece in pieces],
        slot_row,
        mib=16,
    )
    stats, spread = together(stats, spread)
    norms, attended = call(
        merge_body,
        [((SIDE, TILE), F32), far(((TOK, COLS), BF16))],
        quad_one,
        stats,
        arrived,
        mib=16,
    )
    d_key_value, *d_query = call(
        backward_body,
        [far(((2 * TILE, COLS), BF16), HEADS)],
        quad_one,
        far(query, HEADS),
        far(key_value, 2 * HEADS),
        far(grad, HEADS),
        norms,
        mib=24,
        stack=COLS,
    )
    attended = exchange(attended, "z")
    d_key_value, attended = together(d_key_value, attended)
    d_key_value = lax.psum_scatter(d_key_value, "z", scatter_dimension=0, tiled=True)
    spread = fill_spread(attended, spread)
    spread, attended, *d_query[1:4] = together(spread, attended, *d_query[1:4])
    gathered = exchange(spread, QUAD)
    (partial_out,) = call(
        output_body,
        [((4, TOK, SPAN), BF16)],
        attended,
        w_out,
        slot_row,
        mib=16,
    )

    by_core = partial_out.reshape(2, 2, TOK, SPAN)
    summed = pick(by_core, core, 1).astype(F32) + shift(
        pick(by_core, 1 - core, 1), "co", 1, 2
    ).astype(F32)
    half = pick(summed, 1 - y_pos, 0).astype(BF16)
    residual = pick(summed, y_pos, 0) + shift(half, "yh", 1, 2).astype(F32)
    main_mixed = (main_hidden.astype(F32) + residual).astype(BF16)

    (d_w_out,) = call(
        weight_body,
        [far(((COLS, COLS), BF16))],
        gathered,
        mib=16,
    )
    d_w_out, *d_query[4:] = together(d_w_out, *d_query[4:])
    d_query = sum(block.astype(F32) for block in scatter_quad(d_query))
    d_w_out = exchange(d_w_out, "z").reshape(SIDE, COLS // SIDE, COLS)
    d_key, d_value = d_key_value[:TOK], d_key_value[TOK:]
    d_w_out, d_key, d_value = together(d_w_out, d_key, d_value)
    d_w_out = jnp.sum(d_w_out.astype(F32), axis=0).T
    return (
        main_mixed,
        d_query.astype(BF16),
        d_key,
        d_value,
        d_w_out,
    )


def solution(mesh):
    fine = Mesh(mesh.devices.reshape(2, 2, 4, 2, 8), ("yh", "co", "x", "yl", "z"))
    grp, blk = ("yh", "co"), ("x", "yl", "z")
    in_specs = (
        P(blk, grp),
        P(blk, grp),
        P(blk, grp),
        P(blk, grp),
        P(grp, None),
        P(blk, grp),
        P(blk),
    )
    out_specs = (
        P(blk, grp),
        P(blk, grp),
        P(blk, grp),
        P(blk, grp),
        P(grp, blk),
    )
    return jax.shard_map(
        on_device, mesh=fine, in_specs=in_specs, out_specs=out_specs, check_vma=False
    )
```

```python
import math

import jax
import jax.numpy as jnp
from jax import lax
from jax.experimental import pallas as pl
from jax.experimental.pallas import tpu as pltpu
from jax.sharding import Mesh
from jax.sharding import PartitionSpec as P

HD = 128
HEADS = 3
COLS = HEADS * HD
TOK = 128
SIDE = 8
TILE = TOK * SIDE
QB = 256
QF = 1024
SCALE = 1.0 / math.sqrt(HD)
LOG2E = math.log2(math.e)
PEER = TOK // SIDE
SPAN = 768
QUAD = ("x", "yl")
F32 = jnp.float32
BF16 = jnp.bfloat16
NT = (((1,), (1,)), ((), ()))
TN = (((0,), (0,)), ((), ()))
HBM = pl.BlockSpec(memory_space=pltpu.HBM)
VMEM = pl.BlockSpec(memory_space=pltpu.VMEM)
SMEM = pl.BlockSpec(memory_space=pltpu.SMEM)
MIB = 1024 * 1024
STAT = 16
SLAB = TOK + 3 * STAT


def dot(left, right, dims=(((1,), (0,)), ((), ()))):
    return lax.dot_general(left, right, dims, preferred_element_type=F32)


def far(array, parts=1):
    return array, parts


def block_copies(source, dest, sems, first, parts):
    width = source.shape[-1] // parts
    found = []
    for n in range(parts):
        here, there = source, dest
        if parts > 1:
            here, there = (r.at[:, n * width : (n + 1) * width] for r in (source, dest))
        found.append(pltpu.make_async_copy(here, there, sems.at[first + n]))
    return found


def call(body, out, *args, mib, stack=None):
    arg_parts = [arg[1] if isinstance(arg, tuple) else 0 for arg in args]
    args = [arg[0] if isinstance(arg, tuple) else arg for arg in args]
    out_parts = [one[1] if isinstance(one[1], int) else 0 for one in out]
    out = [one[0] if isinstance(one[1], int) else one for one in out]
    n_in, n_out = len(args), len(out)
    far_in = [i for i in range(n_in) if arg_parts[i]]
    far_out = [i for i in range(n_out) if out_parts[i]]
    n_load, n_store = sum(arg_parts), sum(out_parts)

    def kernel(*refs):
        ins, outs = list(refs[:n_in]), list(refs[n_in : n_in + n_out])
        rest = list(refs[n_in + n_out :])
        if stack:
            pieces, rest = rest[:SIDE], rest[SIDE:]
            piece_sem, whole = rest.pop(), rest.pop()
            outs.append(whole)
        loads, stores = {}, {}
        load_sem = rest.pop(0) if n_load else None
        store_sem = rest.pop(0) if n_store else None
        first = 0
        for i in far_in:
            spot = rest.pop(0)
            loads[i] = block_copies(ins[i], spot, load_sem, first, arg_parts[i])
            first += arg_parts[i]
            ins[i] = spot
        first = 0
        for i in far_out:
            spot = rest.pop(0)
            stores[i] = block_copies(spot, outs[i], store_sem, first, out_parts[i])
            first += out_parts[i]
            outs[i] = spot
        for n in range(max(arg_parts)):
            for i in far_in:
                if n < arg_parts[i]:
                    loads[i][n].start()
        for i in far_in:
            if arg_parts[i] == 1:
                loads[i][0].wait()
        started = set()

        def ready(i, n):
            loads[i][n].wait()

        def done(i, n):
            stores[i][n].start()
            started.add((i, n))

        steps = (ready, done) if max(arg_parts) > 1 or max(out_parts) > 1 else ()
        body(*steps, *ins, *outs, *rest)
        for i in far_out:
            for n in range(out_parts[i]):
                if (i, n) not in started:
                    stores[i][n].start()
        if stack:
            stores[n_out] = [
                pltpu.make_async_copy(
                    whole.at[rows_of(around(ins[0][0], step)), :], piece, piece_sem.at[step]
                )
                for step, piece in enumerate(pieces)
            ]
            for copy in stores[n_out]:
                copy.start()
        for i in stores:
            for copy in stores[i]:
                copy.wait()

    dma = pltpu.SemaphoreType.DMA
    return pl.pallas_call(
        kernel,
        out_shape=[
            pltpu.HBM(*one) if out_parts[i] else jax.ShapeDtypeStruct(*one)
            for i, one in enumerate(out)
        ]
        + ([pltpu.HBM((TOK, stack), BF16)] * SIDE if stack else []),
        in_specs=[
            HBM if arg_parts[i] else SMEM if args[i].shape == (1,) else VMEM for i in range(n_in)
        ],
        out_specs=[HBM if parts else VMEM for parts in out_parts] + ([HBM] * SIDE if stack else []),
        scratch_shapes=[
            *([dma((n_load,))] if n_load else []),
            *([dma((n_store,))] if n_store else []),
            *[pltpu.VMEM(args[i].shape, args[i].dtype) for i in far_in],
            *[pltpu.VMEM(*out[i]) for i in far_out],
            *([pltpu.VMEM((TILE, stack), BF16), dma((SIDE,))] if stack else []),
        ],
        compiler_params=pltpu.CompilerParams(vmem_limit_bytes=mib * MIB),
    )(
        *[
            pltpu.with_memory_space_constraint(arg, pltpu.HBM) if arg_parts[i] else arg
            for i, arg in enumerate(args)
        ]
    )


def around(pos, step):
    return lax.rem(pos + (step + SIDE), SIDE)


def rows_of(pos, rows=TOK):
    return pl.ds(pl.multiple_of(pos * rows, rows), rows)


def head(idx):
    return slice(idx * HD, (idx + 1) * HD)


def block_of(slot):
    return (slot >> 7) & (SIDE - 1)


def sorted_by_block(slot_row):
    first = lax.broadcasted_iota(jnp.int32, (TOK, TOK), 0)
    second = lax.broadcasted_iota(jnp.int32, (TOK, TOK), 1)
    spread = jnp.where(first == second, slot_row.astype(F32), 0.0)
    slot_col = jnp.sum(spread, axis=1, keepdims=True).astype(jnp.int32)
    same = (block_of(slot_row) == block_of(slot_col)) & (first < second)
    ahead = jnp.sum(jnp.where(same, 1.0, 0.0), axis=0, keepdims=True).astype(jnp.int32)
    rank = block_of(slot_row) * PEER + ahead
    order = jnp.where(first == rank, 1.0, 0.0).astype(BF16)
    place = jnp.where(
        second == 0,
        (slot_col >> 10).astype(F32),
        jnp.where(second == 1, (slot_col & (TOK - 1)).astype(F32), 0.0),
    )
    return order, place


def project_body(
    y_ref, core_ref, d0_ref, d1_ref, d2_ref, d3_ref, w_ref, row_ref, pay_ref
):
    y_pos, core = y_ref[0], core_ref[0]
    order, place = sorted_by_block(row_ref[...])
    total = jnp.zeros((TOK, COLS), F32)
    pieces = (
        (d0_ref, y_pos, core),
        (d1_ref, 1 - y_pos, core),
        (d2_ref, y_pos, 1 - core),
        (d3_ref, 1 - y_pos, 1 - core),
    )
    for d_ref, along, across in pieces:
        part = 2 * along + across
        here = pl.ds(pl.multiple_of(part * SPAN, SPAN), SPAN)
        total += dot(d_ref[...], w_ref[:, here], NT)
    pay_ref[:, :COLS] = dot(order, total.astype(BF16)).astype(BF16)
    pay_ref[:, COLS:] = dot(order, place.astype(BF16)).astype(BF16)


def cut_body(y_ref, core_ref, d0_ref, d1_ref, d2_ref, d3_ref, row_ref, cut_ref):
    order, _ = sorted_by_block(row_ref[...])
    y_pos, core = y_ref[0], core_ref[0]
    pieces = (
        (d0_ref, y_pos, core),
        (d1_ref, 1 - y_pos, core),
        (d2_ref, y_pos, 1 - core),
        (d3_ref, 1 - y_pos, 1 - core),
    )
    for d_ref, along, across in pieces:
        part = 2 * along + across
        rows = dot(order, d_ref[...]).astype(BF16)
        cut_ref[2 * part, :, COLS:] = rows[:, :COLS]
        cut_ref[2 * part + 1, :, COLS:] = rows[:, COLS:]


def forward_body(ready, done, x_ref, kv_ref, *rest):
    blocks, (q_ref, out_ref, lse_ref) = rest[:-3], rest[-3:]
    for step, block_ref in enumerate(blocks):
        q_ref[rows_of(lax.rem(x_ref[0] + (4 - step), 4), 2 * TOK), :] = block_ref[...]
    for idx in range(HEADS):
        done(0, idx)
    lse_ref[...] = jnp.zeros_like(lse_ref)
    for idx in range(HEADS):
        ready(1, idx)
        ready(1, HEADS + idx)
        keys = kv_ref[:, head(idx)]
        values_t = kv_ref[:, head(HEADS + idx)].T
        for start in range(0, TILE, QF):
            cols = slice(start, start + QF)
            scores = dot(keys, q_ref[cols, head(idx)], NT)
            peak = jnp.max(scores, axis=0, keepdims=True)
            weights = jnp.exp2((scores - peak) * (SCALE * LOG2E))
            total = jnp.sum(weights, axis=0, keepdims=True)
            out_ref[head(idx), cols] = (dot(values_t, weights.astype(BF16)) / total).astype(BF16)
            lse_ref[idx : idx + 1, cols] = peak * SCALE + jnp.log(total)


def places(arrived):
    place = arrived.astype(F32)
    target = place[:, 0:1] * float(TOK) + place[:, 1:2]
    lanes = lax.broadcasted_iota(jnp.int32, (place.shape[0], TILE), 1)
    return jnp.where(lanes == target.astype(jnp.int32), 1.0, 0.0).astype(BF16)


def terms(value, count):
    found = []
    for _ in range(count):
        found.append(value.astype(BF16))
        value = value - found[-1].astype(F32)
    return found


def delta_body(ready, done, arrived_ref, out_ref, lse_ref, grad_ref, send_ref):
    order = places(arrived_ref[:, COLS:])
    deltas = []
    for idx in range(HEADS):
        grad_t = dot(arrived_ref[:, head(idx)].T, order)
        grad_ref[:, head(idx)] = grad_t.T.astype(BF16)
        done(0, idx)
        deltas.append(jnp.sum(grad_t * out_ref[head(idx), :].astype(F32), axis=0, keepdims=True))
        rows = dot(out_ref[head(idx), :], order, NT).T.astype(BF16)
        for peer in range(SIDE):
            send_ref[peer, :TOK, head(idx)] = rows[peer * TOK : (peer + 1) * TOK]
    zero = jnp.zeros((1, TILE), BF16)
    stats = [t for t in terms(lse_ref[:HEADS, :], 3)]
    stats += terms(jnp.concatenate(deltas, axis=0), 2)
    stats = jnp.concatenate([t.astype(F32) for t in stats] + [zero.astype(F32)], axis=0).astype(BF16)
    for peer in range(SIDE):
        for n, start in enumerate(range(0, TILE, COLS)):
            width = min(COLS, TILE - start)
            send_ref[peer, TOK + STAT * n : TOK + STAT * (n + 1), :width] = stats[:, start : start + width]


def merge_body(quad_ref, all_ref, arrived_ref, norm_ref, att_ref):
    lses, deltas = [], []
    for peer in range(SIDE):
        parts = []
        for n, start in enumerate(range(0, TILE, COLS)):
            width = min(COLS, TILE - start)
            parts.append(all_ref[peer, TOK + STAT * n : TOK + STAT * (n + 1), :width].astype(F32))
        stats = jnp.concatenate(parts, axis=1)
        lses.append(stats[0:3] + stats[3:6] + stats[6:9])
        deltas.append(stats[9:12] + stats[12:15])
    peak = lses[0]
    for one in lses[1:]:
        peak = jnp.maximum(peak, one)
    weights = [jnp.exp(one - peak) for one in lses]
    total = sum(weights)
    norm_ref[...] = jnp.zeros_like(norm_ref)
    norm_ref[:HEADS, :] = peak + jnp.log(total)
    norm_ref[HEADS : 2 * HEADS, :] = sum(w * d for w, d in zip(weights, deltas)) / total
    shares = jnp.concatenate([w / total for w in weights], axis=0)
    mine = places(arrived_ref[rows_of(quad_ref[0]), COLS:])
    shares = sum(dot(mine, term, NT) for term in terms(shares, 2))
    for idx in range(HEADS):
        out = jnp.zeros((TOK, HD), F32)
        for peer in range(SIDE):
            col = HEADS * peer + idx
            out += all_ref[peer, :TOK, head(idx)].astype(F32) * shares[:, col : col + 1]
        att_ref[:, head(idx)] = out.astype(BF16)


def backward_body(ready, done, quad_ref, q_ref, kv_ref, grad_ref, norm_ref, dkv_ref, dq_ref):
    for idx in range(HEADS):
        ready(1, idx)
        ready(2, idx)
        ready(2, HEADS + idx)
        ready(3, idx)
        keys = kv_ref[:, head(idx)]
        keys_t = keys.T
        values = kv_ref[:, head(HEADS + idx)]
        d_keys = jnp.zeros((TILE, HD), F32)
        d_values = jnp.zeros((TILE, HD), F32)
        for start in range(0, TILE, QB):
            cols = slice(start, start + QB)
            query = q_ref[cols, head(idx)]
            grad = grad_ref[cols, head(idx)]
            scores = dot(keys, query, NT) * SCALE
            weights = jnp.exp2((scores - norm_ref[idx : idx + 1, cols]) * LOG2E)
            d_probs = dot(values, grad, NT)
            d_scores = weights * (d_probs - norm_ref[HEADS + idx : HEADS + idx + 1, cols])
            d_scores = d_scores.astype(BF16)
            d_values += dot(weights.astype(BF16), grad)
            d_keys += dot(d_scores, query)
            dq_ref[cols, head(idx)] = (dot(keys_t, d_scores) * SCALE).T.astype(BF16)
        d_keys = (d_keys * SCALE).astype(BF16)
        d_values = d_values.astype(BF16)
        for peer in range(SIDE):
            rows = slice(peer * TOK, (peer + 1) * TOK)
            first = 2 * peer * TOK
            dkv_ref[first : first + TOK, head(idx)] = d_keys[rows]
            dkv_ref[first + TOK : first + 2 * TOK, head(idx)] = d_values[rows]
        done(0, idx)


def output_body(sorted_ref, w_ref, row_ref, part_ref):
    order, _ = sorted_by_block(row_ref[...])
    attended = dot(order, sorted_ref[...], TN).astype(BF16)
    for part in range(4):
        part_ref[part] = dot(attended, w_ref[:, part * SPAN : (part + 1) * SPAN]).astype(BF16)


def weight_body(both_ref, out_ref):
    both = both_ref[...].reshape(TILE, 2 * COLS)
    total = dot(both[:, COLS:], both[:, :COLS], TN)
    out_ref[...] = total.astype(BF16)


def fill_spread(attended, spread):
    def kernel(held, _, out_ref, sems):
        copies = [
            pltpu.make_async_copy(held, out_ref.at[peer, :, :COLS], sems.at[peer])
            for peer in range(SIDE)
        ]
        for copy in copies:
            copy.start()
        for copy in copies:
            copy.wait()

    return pl.pallas_call(
        kernel,
        out_shape=pltpu.HBM(spread.shape, spread.dtype),
        in_specs=[VMEM, HBM],
        out_specs=HBM,
        input_output_aliases={1: 0},
        scratch_shapes=[pltpu.SemaphoreType.DMA((SIDE,))],
    )(attended, pltpu.with_memory_space_constraint(spread, pltpu.HBM))


def shift(value, axis, step, size):
    return lax.ppermute(value, axis, [(i, (i + step) % size) for i in range(size)])


def exchange(value, axis):
    return lax.all_to_all(value, axis, split_axis=0, concat_axis=0, tiled=True)


def scatter_quad(blocks):
    return [blocks[0]] + [shift(blocks[step], QUAD, step, SIDE) for step in range(1, SIDE)]


def pick(value, idx, axis):
    return lax.dynamic_index_in_dim(value, idx, axis, keepdims=False)


def together(*values):
    return lax.optimization_barrier(values)


def on_device(main_hidden, ctrl_query, ctrl_key, ctrl_value, w_out, d_mixed, control_slot):
    y_pos, core = lax.axis_index("yh"), lax.axis_index("co")
    x_one = lax.axis_index("x").reshape(1).astype(jnp.int32)
    quad = lax.axis_index("x") * 2 + lax.axis_index("yl")
    slot_row = control_slot.reshape(1, TOK)
    y_one, core_one, quad_one = (p.reshape(1).astype(jnp.int32) for p in (y_pos, core, quad))

    key_value = jnp.concatenate([ctrl_key, ctrl_value], axis=1)
    key_value = lax.all_gather(key_value, "z", axis=0, tiled=True)
    along = shift(d_mixed, "yh", 1, 2)
    near = shift(ctrl_query, "yl", 1, 2)
    d_later, near = together(d_mixed, near)
    across = shift(d_later, "co", 1, 2)
    y_low = lax.axis_index("yl")
    near = jnp.where(
        y_low == 0, jnp.stack([ctrl_query, near]), jnp.stack([near, ctrl_query])
    ).reshape(2 * TOK, COLS)
    both = shift(along, "co", 1, 2)
    (payload,) = call(
        project_body,
        [far(((TOK, COLS + HD), BF16))],
        y_one,
        core_one,
        far(d_mixed),
        along,
        across,
        both,
        far(w_out),
        slot_row,
        mib=16,
    )
    payload, near = together(payload, near)
    payload = exchange(payload, "z")
    query = [near] + [shift(near, "x", step, 4) for step in range(1, 4)]
    payload, *query = together(jnp.tile(payload, (SIDE, 1)), *query)
    arrived = exchange(payload, QUAD)
    query, out_t, lse = call(
        forward_body,
        [far(((TILE, COLS), BF16), HEADS), ((COLS, TILE), BF16), ((SIDE, TILE), F32)],
        x_one,
        far(key_value, 2 * HEADS),
        *[far(block) for block in query],
        mib=40,
    )
    grad, send = call(
        delta_body,
        [far(((TILE, COLS), BF16), HEADS), far(((SIDE, SLAB, COLS), BF16))],
        arrived,
        out_t,
        lse,
        mib=24,
    )
    stats = exchange(send, QUAD)
    send, *pieces = together(send, d_mixed, along, across, both)
    (spread,) = call(
        cut_body,
        [far(((SIDE, TOK, 2 * COLS), BF16))],
        y_one,
        core_one,
        *[far(piece) for piece in pieces],
        slot_row,
        mib=16,
    )
    stats, spread = together(stats, spread)
    norms, attended = call(
        merge_body,
        [((SIDE, TILE), F32), far(((TOK, COLS), BF16))],
        quad_one,
        stats,
        arrived,
        mib=16,
    )
    d_key_value, *d_query = call(
        backward_body,
        [far(((2 * TILE, COLS), BF16), HEADS)],
        quad_one,
        far(query, HEADS),
        far(key_value, 2 * HEADS),
        far(grad, HEADS),
        norms,
        mib=24,
        stack=COLS,
    )
    attended = exchange(attended, "z")
    d_key_value, attended = together(d_key_value, attended)
    d_key_value = lax.psum_scatter(d_key_value, "z", scatter_dimension=0, tiled=True)
    spread = fill_spread(attended, spread)
    spread, attended, *d_query[1:4] = together(spread, attended, *d_query[1:4])
    gathered = exchange(spread, QUAD)
    (partial_out,) = call(
        output_body,
        [((4, TOK, SPAN), BF16)],
        attended,
        w_out,
        slot_row,
        mib=16,
    )

    by_core = partial_out.reshape(2, 2, TOK, SPAN)
    summed = pick(by_core, core, 1).astype(F32) + shift(
        pick(by_core, 1 - core, 1), "co", 1, 2
    ).astype(F32)
    half = pick(summed, 1 - y_pos, 0).astype(BF16)
    residual = pick(summed, y_pos, 0) + shift(half, "yh", 1, 2).astype(F32)
    main_mixed = (main_hidden.astype(F32) + residual).astype(BF16)

    (d_w_out,) = call(
        weight_body,
        [far(((COLS, COLS), BF16))],
        gathered,
        mib=16,
    )
    d_w_out, *d_query[4:] = together(d_w_out, *d_query[4:])
    d_query = sum(block.astype(F32) for block in scatter_quad(d_query))
    d_w_out = exchange(d_w_out, "z").reshape(SIDE, COLS // SIDE, COLS)
    d_key, d_value = d_key_value[:TOK], d_key_value[TOK:]
    d_w_out, d_key, d_value = together(d_w_out, d_key, d_value)
    d_w_out = jnp.sum(d_w_out.astype(F32), axis=0).T
    return (
        main_mixed,
        d_query.astype(BF16),
        d_key,
        d_value,
        d_w_out,
    )


def solution(mesh):
    fine = Mesh(mesh.devices.reshape(2, 2, 4, 2, 8), ("yh", "co", "x", "yl", "z"))
    grp, blk = ("yh", "co"), ("x", "yl", "z")
    in_specs = (
        P(blk, grp),
        P(blk, grp),
        P(blk, grp),
        P(blk, grp),
        P(grp, None),
        P(blk, grp),
        P(blk),
    )
    out_specs = (
        P(blk, grp),
        P(blk, grp),
        P(blk, grp),
        P(blk, grp),
        P(grp, blk),
    )
    return jax.shard_map(
        on_device, mesh=fine, in_specs=in_specs, out_specs=out_specs, check_vma=False
    )
```
